128 devices in a mesh: dp: 8 (over x, core), expert: 16 (over z, y).
Axes of the slice: x: 4, y: 4, z: 4, core: 2. Of those that a mesh axis runs over, the one named last changes fastest.
Arguments:
- tokens: bfloat16 [128, 197, 768], P(('dp', 'expert')), may hold values from -6 to 6
- norm_attn_a: bfloat16 [768], P('dp'), may hold values from 0.5 to 1.5
- in_proj_a: bfloat16 [768, 2304], P('dp'), may hold values from -0.21875 to 0.21875
- out_proj_a: bfloat16 [768, 768], P('dp'), may hold values from -1.25 to 1.25
- norm_dense: bfloat16 [768], P('dp'), may hold values from 0.5 to 1.5
- dense_up: bfloat16 [768, 3072], P('dp'), may hold values from -0.21875 to 0.21875
- dense_down: bfloat16 [3072, 768], P('dp'), may hold values from -0.109375 to 0.109375
- norm_attn_b: bfloat16 [768], P('dp'), may hold values from 0.5 to 1.5
- in_proj_b: bfloat16 [768, 2304], P('dp'), may hold values from -0.21875 to 0.21875
- out_proj_b: bfloat16 [768, 768], P('dp'), may hold values from -1.25 to 1.25
- norm_moe: bfloat16 [768], P('dp'), may hold values from 0.5 to 1.5
- router: bfloat16 [768, 16], P('dp'), may hold values from -0.15625 to 0.15625
- expert_up: bfloat16 [16, 768, 3072], P('expert', None, 'dp'), may hold values from -0.21875 to 0.21875
- expert_down: bfloat16 [16, 3072, 768], P('expert', 'dp'), may hold values from -0.875 to 0.875
- routes: int32 [128, 197, 2], P(('dp', 'expert')), may hold values from 0 to 15, as said below
- slot_index: int32 [128, 197, 2], P(('dp', 'expert')), may hold values from 0 to 29, as said below
- keep_mask: int32 [128, 197, 2], P(('dp', 'expert')), may hold values 0 or 1
- output_grad: bfloat16 [128, 197, 768], P(('dp', 'expert')), may hold values from -6 to 6
Outputs:
- output: bfloat16 [128, 197, 768], P(('dp', 'expert'))
- input_grad: float32 [128, 197, 768], P(('dp', 'expert'))
- grad_norm_attn_a: float32 [768], P('dp')
- grad_in_proj_a: float32 [768, 2304], P('dp')
- grad_out_proj_a: float32 [768, 768], P('dp')
- grad_norm_dense: float32 [768], P('dp')
- grad_dense_up: float32 [768, 3072], P('dp')
- grad_dense_down: float32 [3072, 768], P('dp')
- grad_norm_attn_b: float32 [768], P('dp')
- grad_in_proj_b: float32 [768, 2304], P('dp')
- grad_out_proj_b: float32 [768, 768], P('dp')
- grad_norm_moe: float32 [768], P('dp')
- grad_router: float32 [768, 16], P('dp')
- grad_expert_up: float32 [16, 768, 3072], P('expert', None, 'dp')
- grad_expert_down: float32 [16, 3072, 768], P('expert', 'dp')
The draws below stay inside these ranges and needn't reach their ends.
Inputs may be any that keep to these rules, and one draw needn't show every extreme that they name: `routes`: each token names two different experts; of the 197 tokens of one device, at most 15 name an expert as first choice and at most 15 as second. `slot_index`: first choices take slots below 15, second choices slots from 15 on; two choices of one device for one expert never share a slot; every device uses slot 29 of some expert.
All inputs are finite; a program needn't handle non-finite values. No bound on the sum of `keep_mask` on one device may be relied on, other than what follows from the above.
Results may differ from the reference program's by a relative error of at most 0.03.
Values may be sent and summed in bfloat16 or wider, within the bound.
No kernel may reach another device: no remote copies, remote signals or barrier semaphores. Data moves between devices by JAX's collectives and lax.ppermute only.
A program may use at most 192 MiB of HBM per device.

```python
import jax
import jax.numpy as jnp
from jax import lax

D = 768
HEADS = 12
HEAD_DIM = 64
FF = 3072
LEN = 197
SEQ_DEV = 1
EXPERTS = 16
ROWS = 197
SEQS = 128
HALF = 15
CAP = 30
N_DP = 8
N_EXPERT = 16


def route_plan(key):
    devices = SEQS // SEQ_DEV
    slots_all = EXPERTS * HALF
    keys = jax.random.split(jax.random.fold_in(key, 11), 3)
    forced = jax.random.randint(keys[0], (devices, 1), 0, EXPERTS)
    slot_ids = jnp.arange(slots_all, dtype=jnp.int32)[None, :]
    noise = jax.random.randint(keys[1], (devices, slots_all), 0, 1 << 20)
    score = jnp.where(slot_ids // HALF == forced, 0, noise + 1) * slots_all + slot_ids
    chosen = jnp.argsort(score, axis=1)[:, :ROWS].astype(jnp.int32)
    token_ids = jnp.arange(ROWS, dtype=jnp.int32)[None, :]
    order_noise = jax.random.randint(keys[2], (devices, ROWS), 0, 1 << 20)
    shuffle = jnp.argsort(order_noise * ROWS + token_ids, axis=1).astype(jnp.int32)
    first_slot = jnp.take_along_axis(chosen, shuffle, axis=1)
    first_expert = first_slot // HALF
    first_place = first_slot % HALF
    ranked = jnp.argsort(first_expert * ROWS + token_ids, axis=1).astype(jnp.int32)
    partner = jnp.roll(ranked, -HALF, axis=1)
    second_expert_ranked = jnp.take_along_axis(first_expert, partner, axis=1)
    second_place_ranked = jnp.take_along_axis(first_place, partner, axis=1)
    inverse = jnp.argsort(ranked, axis=1).astype(jnp.int32)
    second_expert = jnp.take_along_axis(second_expert_ranked, inverse, axis=1)
    second_place = jnp.take_along_axis(second_place_ranked, inverse, axis=1)
    experts_out = jnp.stack([first_expert, second_expert], axis=-1).reshape(SEQS, LEN, 2)
    slots_out = jnp.stack([first_place, HALF + second_place], axis=-1).reshape(SEQS, LEN, 2)
    return (experts_out.astype(jnp.int32), slots_out.astype(jnp.int32))


def draw_routes(key, part):
    experts_out, slots_out = route_plan(key)
    return experts_out


def draw_slot_index(key, part):
    experts_out, slots_out = route_plan(key)
    return slots_out


def set_ends(array, rng, smallest, top_value):
    shape = array.shape
    spot = [jax.random.randint(jax.random.fold_in(rng, axis), (), 0, shape[axis]) for axis in range(len(shape))]
    array = array.at[tuple(spot)].set(smallest)
    longest = shape.index(max(shape))
    spot[longest] = (spot[longest] + 1) % shape[longest]
    return array.at[tuple(spot)].set(top_value)


def block_levels(key, dims, cuts, low, high):
    level, own = 1.0, jax.random.fold_in(key, 6)
    for axis_at, blocks in cuts:
        draws = jnp.exp(jax.random.uniform(jax.random.fold_in(own, axis_at), (blocks,), jnp.float32, low / len(cuts), high / len(cuts)))
        level = level * jnp.repeat(draws, dims[axis_at] // blocks).reshape([-1 if axis == axis_at else 1 for axis in range(len(dims))])
    return level


def scatter_about(key, dims, deviation, bound, shards=(), held_as=jnp.bfloat16):
    result = jax.random.normal(key, dims, jnp.float32) * deviation
    if len(shards) > 0:
        result = block_levels(key, dims, shards, -0.22, 0.18) * result
    return jnp.clip(result, min=-bound, max=bound).astype(held_as)


def setup_inputs(seed: int = 0) -> dict:
    key_list = jax.random.split(jax.random.key(seed), 19)
    tokens = scatter_about(key_list[0], (SEQS, LEN, D), 1.0, 6.0, ((0, 128),))
    norm_attn_a = jnp.clip(1.0 + 0.1 * jax.random.normal(key_list[1], (D,), jnp.float32), 0.5, 1.5).astype(jnp.bfloat16)
    in_proj_a = scatter_about(key_list[2], (D, 3 * D), D ** -0.5, 0.21875, ((0, 8),))
    out_proj_a = scatter_about(key_list[3], (D, D), (D // 32) ** -0.5, 1.25, ((0, 8),))
    norm_dense = jnp.clip(1.0 + 0.1 * jax.random.normal(key_list[4], (D,), jnp.float32), 0.5, 1.5).astype(jnp.bfloat16)
    dense_up = scatter_about(key_list[5], (D, FF), D ** -0.5, 0.21875, ((0, 8),))
    dense_down = scatter_about(key_list[6], (FF, D), FF ** -0.5, 0.109375, ((0, 8),))
    norm_attn_b = jnp.clip(1.0 + 0.1 * jax.random.normal(key_list[7], (D,), jnp.float32), 0.5, 1.5).astype(jnp.bfloat16)
    in_proj_b = scatter_about(key_list[8], (D, 3 * D), D ** -0.5, 0.21875, ((0, 8),))
    out_proj_b = scatter_about(key_list[9], (D, D), (D // 32) ** -0.5, 1.25, ((0, 8),))
    norm_moe = jnp.clip(1.0 + 0.1 * jax.random.normal(key_list[10], (D,), jnp.float32), 0.5, 1.5).astype(jnp.bfloat16)
    router = scatter_about(key_list[11], (D, EXPERTS), (2 * D) ** -0.5, 0.15625, ((0, 8),))
    expert_up = scatter_about(key_list[12], (EXPERTS, D, FF), D ** -0.5, 0.21875, ((0, 16), (2, 8)))
    expert_down = scatter_about(key_list[13], (EXPERTS, FF, D), (FF // 64) ** -0.5, 0.875, ((0, 16), (1, 8)))
    routes = draw_routes(jax.random.fold_in(key_list[18], 71), 0)
    slot_index = draw_slot_index(jax.random.fold_in(key_list[18], 71), 0)
    keep_mask = set_ends((jax.random.randint(key_list[16], (SEQS, LEN, 2), 0, 8) < 7).astype(jnp.int32), jax.random.fold_in(key_list[16], 1), 0, 1)
    output_grad = scatter_about(key_list[17], (SEQS, LEN, D), 1.0, 6.0, ((0, 128),))
    return dict(tokens=tokens, norm_attn_a=norm_attn_a, in_proj_a=in_proj_a, out_proj_a=out_proj_a, norm_dense=norm_dense, dense_up=dense_up, dense_down=dense_down, norm_attn_b=norm_attn_b, in_proj_b=in_proj_b, out_proj_b=out_proj_b, norm_moe=norm_moe, router=router, expert_up=expert_up, expert_down=expert_down, routes=routes, slot_index=slot_index, keep_mask=keep_mask, output_grad=output_grad)


@jax.custom_vjp
def low(v):
    return lax.optimization_barrier(v.astype(jnp.bfloat16)).astype(jnp.float32)

@jax.custom_vjp
def low_back(v):
    return v

def low_keep(v):
    return (low(v), None)

def low_pass(kept, grad):
    return (grad,)

def back_keep(v):
    return (v, None)

def back_low(kept, grad):
    return (low(grad),)
low.defvjp(low_keep, low_pass)
low_back.defvjp(back_keep, back_low)
exact_precision = lax.Precision.HIGHEST
epsilon = 1e-06

def matmul(left, right):
    return jnp.dot(left, right, precision=exact_precision, preferred_element_type=jnp.float32)

def norm_rows(stream, gain):
    center = lax.optimization_barrier(jnp.mean(stream, axis=-1, keepdims=True))
    centred = stream - center
    spread = lax.optimization_barrier(jnp.mean(centred * centred, axis=-1, keepdims=True))
    return centred * lax.rsqrt(spread + epsilon) * gain

def softmax_rows(scores):
    top = lax.optimization_barrier(jnp.max(scores, axis=-1, keepdims=True))
    expo = jnp.exp(scores - top)
    return expo / lax.optimization_barrier(jnp.sum(expo, axis=-1, keepdims=True))

def attend_image(joined):
    query, key, value = (joined[:, 0], joined[:, 1], joined[:, 2])
    scale = HEAD_DIM ** (-0.5)
    scores = jnp.einsum('qhd,khd->hqk', query, key, precision=exact_precision) * scale
    scores = low_back(scores)
    weights = low(softmax_rows(scores))
    return jnp.einsum('hqk,khd->qhd', weights, value, precision=exact_precision)

def attention(stream, gain, in_proj, out_proj):
    normed = low(norm_rows(stream, gain))
    joined = low(low_back(matmul(normed, in_proj)))
    joined = joined.reshape(SEQS, LEN, 3, HEADS, HEAD_DIM)
    mixed = lax.map(jax.checkpoint(attend_image), joined)
    mixed = low(low_back(mixed.reshape(SEQS * LEN, D)))
    return stream + low_back(matmul(mixed, out_proj))

def dense_block(stream, gain, up_w, down_w):
    normed = low(norm_rows(stream, gain))
    pre = low_back(matmul(normed, up_w))
    hidden = low(jax.nn.gelu(pre, approximate=False))
    return stream + low_back(matmul(hidden, down_w))

def run_expert(pieces):
    rows_in, up_w, down_w = pieces
    pre = low_back(matmul(rows_in, up_w))
    hidden = low(jax.nn.gelu(pre, approximate=False))
    return low(low_back(matmul(hidden, down_w)))

def expert_block(stream, gain, router, up_w, down_w, flat_routes, place, keep):
    normed = low(norm_rows(stream, gain))
    logits = low_back(matmul(normed, router))
    probs = softmax_rows(logits)
    gates = jnp.take_along_axis(probs, flat_routes, axis=1) * keep
    buffer = jnp.zeros((EXPERTS, N_DP * N_EXPERT * CAP, D), jnp.float32)
    buffer = buffer.at[flat_routes[:, 0], place[:, 0]].add(normed * keep[:, 0:1])
    buffer = buffer.at[flat_routes[:, 1], place[:, 1]].add(normed * keep[:, 1:2])
    buffer = low_back(buffer)
    results = lax.map(jax.checkpoint(run_expert), (buffer, up_w, down_w))
    first = results[flat_routes[:, 0], place[:, 0]]
    second = results[flat_routes[:, 1], place[:, 1]]
    return stream + gates[:, 0:1] * first + gates[:, 1:2] * second

def reference(tokens, norm_attn_a, in_proj_a, out_proj_a, norm_dense, dense_up, dense_down, norm_attn_b, in_proj_b, out_proj_b, norm_moe, router, expert_up, expert_down, routes, slot_index, keep_mask, output_grad):
    total = SEQS * LEN
    flat_routes = routes.reshape(total, 2).astype(jnp.int32)
    flat_slots = slot_index.reshape(total, 2).astype(jnp.int32)
    keep = keep_mask.reshape(total, 2).astype(jnp.float32)
    device = (jnp.arange(total, dtype=jnp.int32) // ROWS).astype(jnp.int32)
    place = (device[:, None] * CAP + flat_slots).astype(jnp.int32)
    params = tuple((weight.astype(jnp.float32) for weight in (norm_attn_a, in_proj_a, out_proj_a, norm_dense, dense_up, dense_down, norm_attn_b, in_proj_b, out_proj_b, norm_moe, router, expert_up, expert_down)))
    stream = tokens.reshape(total, D).astype(jnp.float32)

    def forward(stream, params):
        stream = attention(stream, params[0], params[1], params[2])
        stream = dense_block(stream, params[3], params[4], params[5])
        stream = attention(stream, params[6], params[7], params[8])
        return expert_block(stream, params[9], params[10], params[11], params[12], flat_routes, place, keep)
    final, pullback = jax.vjp(forward, stream, params)
    stream_grad, grads = pullback(output_grad.reshape(total, D).astype(jnp.float32))
    output = final.astype(jnp.bfloat16).reshape(SEQS, LEN, D)
    input_grad = stream_grad.reshape(SEQS, LEN, D)
    return (output, input_grad, grads[0], grads[1], grads[2], grads[3], grads[4], grads[5], grads[6], grads[7], grads[8], grads[9], grads[10], grads[11], grads[12])
```

```python
import math

import jax
import jax.numpy as jnp
from jax import lax
from jax.sharding import Mesh, PartitionSpec as P

HEAD_DIM = 64


epsilon = 1e-06


def product(left, right):
    return jnp.dot(left, right, preferred_element_type=jnp.float32)


def product_t(left, right):
    return lax.dot_general(
        left, right, (((0,), (0,)), ((), ())), preferred_element_type=jnp.float32
    )


def product_bt(left, right):
    return lax.dot_general(
        left, right, (((1,), (1,)), ((), ())), preferred_element_type=jnp.float32
    )


def norm_rows(stream, gain):
    center = jnp.mean(stream, axis=-1, keepdims=True)
    centred = stream - center
    spread = jnp.mean(centred * centred, axis=-1, keepdims=True)
    inverse = lax.rsqrt(spread + epsilon)
    scaled = centred * inverse
    return (scaled * gain.astype(jnp.float32), (scaled, inverse))


def norm_back(grad, gain, saved):
    scaled, inverse = saved
    shifted = grad * gain.astype(jnp.float32)
    gain_grad = jnp.sum(grad * scaled, axis=0)
    inner = (
        shifted
        - jnp.mean(shifted, axis=-1, keepdims=True)
        - scaled * jnp.mean(shifted * scaled, axis=-1, keepdims=True)
    )
    return (inner * inverse, gain_grad)


def gelu_parts(value):
    normal_cdf = 0.5 * (1.0 + lax.erf(value * (1.0 / math.sqrt(2.0))))
    slope = normal_cdf + value * jnp.exp(-0.5 * value * value) * (1.0 / math.sqrt(2.0 * math.pi))
    return value * normal_cdf, slope


def split_heads(joined, images, length):
    heads = joined.shape[1] // (3 * HEAD_DIM)
    parts = joined.reshape(images, length, 3, heads, HEAD_DIM)
    return (parts[:, :, 0], parts[:, :, 1], parts[:, :, 2])


X, CORES = 4, 2
SLOTS = 32


def x_shift(block, step):
    return lax.ppermute(block, "x", [(i, (i + step) % X) for i in range(X)])


def core_swap(block):
    return lax.ppermute(block, "core", [(0, 1), (1, 0)])


def gather_rows(shard):
    xi, ci = lax.axis_index("x"), lax.axis_index("core")
    half = jnp.zeros((X,) + shard.shape, shard.dtype)
    half = lax.dynamic_update_index_in_dim(half, shard, xi, 0)
    for step in range(1, X):
        half = lax.dynamic_update_index_in_dim(half, x_shift(shard, step), (xi - step) % X, 0)
    other = core_swap(half)
    whole = jnp.where(
        ci == 0, jnp.stack([half, other], axis=1), jnp.stack([other, half], axis=1)
    )
    return whole.reshape(X * CORES * shard.shape[0], shard.shape[1])


def split_rows(left):
    xi, ci = lax.axis_index("x"), lax.axis_index("core")
    rows, wide = left.shape
    blocks = left.T.reshape(X, CORES, wide // (X * CORES), rows)
    blocks = lax.dynamic_slice_in_dim(jnp.concatenate([blocks, blocks], axis=0), xi, X, axis=0)
    own = lax.dynamic_index_in_dim(blocks, ci, 1, keepdims=False)
    other = lax.dynamic_index_in_dim(blocks, 1 - ci, 1, keepdims=False)
    return own.reshape(wide // CORES, rows), other.reshape(wide // CORES, rows)


def sum_over_x(first, blocks, sign):
    total = first
    for step in range(1, X):
        total = total + x_shift(blocks[step - 1], sign * step).astype(jnp.float32)
    return total


def scatter_halves(own, other):
    total = own + core_swap(other.astype(jnp.bfloat16)).astype(jnp.float32)
    block = own.shape[0] // X
    low = total[block:].astype(jnp.bfloat16)
    return sum_over_x(total[:block], [low[k * block : (k + 1) * block] for k in range(X - 1)], 1)


def weight_grad(left, right):
    own, other = split_rows(left)
    return scatter_halves(product(own, right), product(other, right))


def attend_forward(stream, gain, in_proj, out_proj, images, length):
    rows, width = stream.shape
    scale = HEAD_DIM ** (-0.5)
    normed_f, saved = norm_rows(stream, gain)
    normed = normed_f.astype(jnp.bfloat16)
    joined = product(normed, in_proj).astype(jnp.bfloat16)
    query, key, value = split_heads(joined, images, length)
    scores = jnp.einsum("sqhd,skhd->shqk", query, key, preferred_element_type=jnp.float32) * scale
    top = jnp.max(scores, axis=-1, keepdims=True)
    expo = jnp.exp(scores - top)
    total = jnp.sum(expo, axis=-1, keepdims=True)
    weights = expo / total
    log_total = top + jnp.log(total)
    mixed = jnp.einsum(
        "shqk,skhd->sqhd", weights.astype(jnp.bfloat16), value, preferred_element_type=jnp.float32
    )
    mixed = mixed.reshape(rows, width).astype(jnp.bfloat16)
    return (stream + product(mixed, out_proj), (normed, saved, joined, log_total, mixed))


def attend_backward(grad, gain, in_proj, out_proj, kept, images, length):
    normed, saved, joined, log_total, mixed = kept
    rows, width = grad.shape
    scale = HEAD_DIM ** (-0.5)
    grad_low = grad.astype(jnp.bfloat16)
    out_grad_w = weight_grad(mixed, grad_low)
    query, key, value = split_heads(joined, images, length)
    mixed_grad = product_bt(grad_low, out_proj).astype(jnp.bfloat16).reshape(query.shape)
    scores = jnp.einsum("sqhd,skhd->shqk", query, key, preferred_element_type=jnp.float32) * scale
    weights = jnp.exp(scores - log_total)
    weight_grad_ = jnp.einsum(
        "sqhd,skhd->shqk", mixed_grad, value, preferred_element_type=jnp.float32
    )
    value_grad = jnp.einsum(
        "shqk,sqhd->skhd",
        weights.astype(jnp.bfloat16),
        mixed_grad,
        preferred_element_type=jnp.float32,
    )
    score_grad = weights * (weight_grad_ - jnp.sum(weights * weight_grad_, axis=-1, keepdims=True))
    score_grad = score_grad.astype(jnp.bfloat16)
    query_grad = (
        jnp.einsum("shqk,skhd->sqhd", score_grad, key, preferred_element_type=jnp.float32) * scale
    )
    key_grad = (
        jnp.einsum("shqk,sqhd->skhd", score_grad, query, preferred_element_type=jnp.float32) * scale
    )
    joined_grad = (
        jnp.stack([query_grad, key_grad, value_grad], axis=2)
        .reshape(rows, 3 * width)
        .astype(jnp.bfloat16)
    )
    in_grad_w = weight_grad(normed, joined_grad)
    stream_grad, gain_grad = norm_back(product_bt(joined_grad, in_proj), gain, saved)
    return (grad + stream_grad, (gain_grad, in_grad_w, out_grad_w))


def dense_forward(stream, gain, up_w, down_w):
    normed_f, saved = norm_rows(stream, gain)
    normed = normed_f.astype(jnp.bfloat16)
    hidden, slope = gelu_parts(product(normed, up_w))
    hidden = hidden.astype(jnp.bfloat16)
    return (stream + product(hidden, down_w), (normed, saved, slope, hidden))


def dense_backward(grad, gain, up_w, down_w, kept):
    normed, saved, slope, hidden = kept
    grad_low = grad.astype(jnp.bfloat16)
    down_grad = weight_grad(hidden, grad_low)
    pre_grad = (product_bt(grad_low, down_w) * slope).astype(jnp.bfloat16)
    up_grad = weight_grad(normed, pre_grad)
    stream_grad, gain_grad = norm_back(product_bt(pre_grad, up_w), gain, saved)
    return (grad + stream_grad, (gain_grad, up_grad, down_grad))


def moe(stream, grad_low, gain, router, up_local, down_local, routes, slot_index, keep_mask):
    rows, width = stream.shape
    experts = router.shape[1]
    slots = experts * SLOTS
    hidden_local = up_local.shape[1]
    grad = grad_low.astype(jnp.float32)
    ups = [up_local] + [x_shift(up_local, k) for k in range(1, X)]
    downs = [down_local] + [x_shift(down_local, k) for k in range(1, X)]
    up_half = jnp.concatenate(ups, axis=1)
    down_half = jnp.concatenate(downs, axis=0)

    normed_f, saved = norm_rows(stream, gain)
    normed = normed_f.astype(jnp.bfloat16)
    logits = product(normed, router)
    top = jnp.max(logits, axis=-1, keepdims=True)
    expo = jnp.exp(logits - top)
    probs = expo / jnp.sum(expo, axis=-1, keepdims=True)
    expert_ids = lax.broadcasted_iota(jnp.int32, (rows, experts), 1)
    keep_float = keep_mask.astype(jnp.float32)
    keep_first, keep_second = keep_float[:, 0:1], keep_float[:, 1:2]
    hot_first = (expert_ids == routes[:, 0:1]).astype(jnp.float32)
    hot_second = (expert_ids == routes[:, 1:2]).astype(jnp.float32)
    gate_first = jnp.sum(probs * hot_first, axis=-1, keepdims=True) * keep_first
    gate_second = jnp.sum(probs * hot_second, axis=-1, keepdims=True) * keep_second
    columns = lax.broadcasted_iota(jnp.int32, (rows, slots), 1)
    target = routes * SLOTS + slot_index
    pick_first = (columns == target[:, 0:1]).astype(jnp.float32) * keep_first
    pick_second = (columns == target[:, 1:2]).astype(jnp.float32) * keep_second
    select = (pick_first + pick_second).astype(jnp.bfloat16)
    slot_gate = jnp.sum(pick_first * gate_first + pick_second * gate_second, axis=0)
    send_rows = product_t(select, normed).astype(jnp.bfloat16)
    send_grad = (product_t(select, grad_low) * slot_gate[:, None]).astype(jnp.bfloat16)
    send = jnp.stack(
        [send_rows.reshape(experts, SLOTS, width), send_grad.reshape(experts, SLOTS, width)], axis=1
    )
    received = lax.all_to_all(send, ("z", "y"), split_axis=0, concat_axis=0, tiled=True)
    partner = core_swap(received)

    flat = jnp.concatenate(
        [received[:, 0].reshape(slots, width), partner[:, 0].reshape(slots, width)], axis=0
    )
    flat_grad = jnp.concatenate(
        [received[:, 1].reshape(slots, width), partner[:, 1].reshape(slots, width)], axis=0
    )
    hidden, slope = gelu_parts(product(flat, up_half))
    hidden = hidden.astype(jnp.bfloat16)
    partial_out = product(hidden, down_half)
    pre_grad = (product_bt(flat_grad, down_half) * slope).astype(jnp.bfloat16)
    partial_in = product_bt(pre_grad, up_half)
    other_half = jnp.stack(
        [
            partial_out[slots:].astype(jnp.bfloat16).reshape(experts, SLOTS, width),
            partial_in[slots:].astype(jnp.bfloat16).reshape(experts, SLOTS, width),
        ],
        axis=1,
    )
    own_half = jnp.stack(
        [
            partial_out[:slots].reshape(experts, SLOTS, width),
            partial_in[:slots].reshape(experts, SLOTS, width),
        ],
        axis=1,
    )
    back = (own_half + core_swap(other_half).astype(jnp.float32)).astype(jnp.bfloat16)
    returned = lax.all_to_all(back, ("z", "y"), split_axis=0, concat_axis=0, tiled=True)
    result_rows = returned[:, 0].reshape(slots, width)
    back_rows = returned[:, 1].reshape(slots, width)

    cuts = [slice(k * hidden_local, (k + 1) * hidden_local) for k in range(X)]
    up_parts = [product_t(flat, pre_grad[:, cut]) for cut in cuts]
    down_parts = [product_t(hidden[:, cut], flat_grad) for cut in cuts]
    up_grad = sum_over_x(up_parts[0], [p.astype(jnp.bfloat16) for p in up_parts[1:]], -1)
    down_grad = sum_over_x(down_parts[0], [p.astype(jnp.bfloat16) for p in down_parts[1:]], -1)

    first = product(pick_first.astype(jnp.bfloat16), result_rows)
    second = product(pick_second.astype(jnp.bfloat16), result_rows)
    new_stream = stream + gate_first * first + gate_second * second
    gate_grad_first = jnp.sum(grad * first, axis=-1, keepdims=True) * keep_first
    gate_grad_second = jnp.sum(grad * second, axis=-1, keepdims=True) * keep_second
    probs_grad = gate_grad_first * hot_first + gate_grad_second * hot_second
    logit_grad = probs * (probs_grad - jnp.sum(probs * probs_grad, axis=-1, keepdims=True))
    logit_grad = logit_grad.astype(jnp.bfloat16)
    router_grad = product_t(normed, logit_grad)
    normed_grad = product_bt(logit_grad, router) + product(select, back_rows)
    stream_grad, gain_grad = norm_back(normed_grad, gain, saved)
    return (new_stream, grad + stream_grad, (gain_grad, router_grad, up_grad, down_grad))


def shards(
    tokens,
    norm_attn_a,
    in_proj_a,
    out_proj_a,
    norm_dense,
    dense_up,
    dense_down,
    norm_attn_b,
    in_proj_b,
    out_proj_b,
    norm_moe,
    router,
    expert_up,
    expert_down,
    routes,
    slot_index,
    keep_mask,
    output_grad,
):
    images, length, width = tokens.shape
    rows = images * length
    stream = tokens.reshape(rows, width).astype(jnp.float32)
    flat_routes = routes.reshape(rows, 2)
    flat_slots = slot_index.reshape(rows, 2)
    flat_keep = keep_mask.reshape(rows, 2)
    experts = router.shape[1]
    small = jnp.concatenate(
        [
            jnp.stack([norm_attn_a, norm_dense, norm_attn_b, norm_moe], axis=1),
            router,
            jnp.zeros((router.shape[0], 128 - 4 - experts), router.dtype),
        ],
        axis=1,
    )
    wide_in, wide_out = in_proj_a.shape[1], out_proj_a.shape[1]
    first = gather_rows(jnp.concatenate([in_proj_a, out_proj_a, small], axis=1))
    in_aa, out_aa = first[:, :wide_in], first[:, wide_in : wide_in + wide_out]
    small_all = first[:, wide_in + wide_out :]
    gain_aa, gain_dd, gain_bb, gain_mm = (small_all[:, k] for k in range(4))
    router_full = small_all[:, 4 : 4 + experts]
    up_dd = gather_rows(dense_up)
    down_dd = gather_rows(dense_down)
    second = gather_rows(jnp.concatenate([in_proj_b, out_proj_b], axis=1))
    in_bb, out_bb = second[:, :wide_in], second[:, wide_in:]

    stream_one, kept_one = attend_forward(stream, gain_aa, in_aa, out_aa, images, length)
    stream_two, kept_two = dense_forward(stream_one, gain_dd, up_dd, down_dd)
    stream_three, kept_three = attend_forward(stream_two, gain_bb, in_bb, out_bb, images, length)
    stream_four, grad, moe_grads = moe(
        stream_three,
        output_grad.reshape(rows, width),
        gain_mm,
        router_full,
        expert_up[0],
        expert_down[0],
        flat_routes,
        flat_slots,
        flat_keep,
    )
    output = stream_four.astype(jnp.bfloat16).reshape(images, length, width)
    grad, attn_b_grads = attend_backward(grad, gain_bb, in_bb, out_bb, kept_three, images, length)
    grad, dense_grads = dense_backward(grad, gain_dd, up_dd, down_dd, kept_two)
    grad, attn_a_grads = attend_backward(grad, gain_aa, in_aa, out_aa, kept_one, images, length)
    input_grad = grad.reshape(images, length, width)
    small_grad = jnp.concatenate(
        [
            jnp.stack([attn_a_grads[0], dense_grads[0], attn_b_grads[0], moe_grads[0]], axis=0),
            moe_grads[1].T,
            jnp.zeros((128 - 4 - experts, width), jnp.float32),
        ],
        axis=0,
    )
    small_share = scatter_halves(*split_rows(small_grad))
    shares = [
        attn_a_grads[1],
        attn_a_grads[2],
        dense_grads[1],
        dense_grads[2],
        attn_b_grads[1],
        attn_b_grads[2],
        small_share,
    ]
    totals = lax.psum([share.astype(jnp.bfloat16) for share in shares], ("z", "y"))
    in_a, out_a, up, down, in_b, out_b, small_total = [t.astype(jnp.float32) for t in totals]
    return (
        output,
        input_grad,
        small_total[:, 0],
        in_a,
        out_a,
        small_total[:, 1],
        up,
        down,
        small_total[:, 2],
        in_b,
        out_b,
        small_total[:, 3],
        small_total[:, 4 : 4 + experts],
        moe_grads[2][None],
        moe_grads[3][None],
    )


def solution(mesh):
    places = Mesh(mesh.devices.reshape(X, CORES, 4, 4), ("x", "core", "z", "y"))
    dp, expert = ("x", "core"), ("z", "y")
    images = P(dp + expert, None, None)
    return jax.shard_map(
        shards,
        mesh=places,
        in_specs=(
            images,
            P(dp),
            P(dp, None),
            P(dp, None),
            P(dp),
            P(dp, None),
            P(dp, None),
            P(dp),
            P(dp, None),
            P(dp, None),
            P(dp),
            P(dp, None),
            P(expert, None, dp),
            P(expert, dp, None),
            images,
            images,
            images,
            images,
        ),
        out_specs=(
            images,
            images,
            P(dp),
            P(dp, None),
            P(dp, None),
            P(dp),
            P(dp, None),
            P(dp, None),
            P(dp),
            P(dp, None),
            P(dp, None),
            P(dp),
            P(dp, None),
            P(expert, None, dp),
            P(expert, dp, None),
        ),
        check_vma=False,
    )
```

```python
import math

import jax
import jax.numpy as jnp
from jax import lax
from jax.experimental import pallas as pl
from jax.experimental.pallas import tpu as pltpu
from jax.sharding import Mesh, PartitionSpec as P

HEAD_DIM = 64


epsilon = 1e-06


def product(left, right):
    return jnp.dot(left, right, preferred_element_type=jnp.float32)


def product_t(left, right):
    return lax.dot_general(
        left, right, (((0,), (0,)), ((), ())), preferred_element_type=jnp.float32
    )


def product_bt(left, right):
    return lax.dot_general(
        left, right, (((1,), (1,)), ((), ())), preferred_element_type=jnp.float32
    )


def norm_rows(stream, gain):
    center = jnp.mean(stream, axis=-1, keepdims=True)
    centred = stream - center
    spread = jnp.mean(centred * centred, axis=-1, keepdims=True)
    inverse = lax.rsqrt(spread + epsilon)
    scaled = centred * inverse
    return (scaled * gain.astype(jnp.float32), (scaled, inverse))


def norm_back(grad, gain, saved):
    scaled, inverse = saved
    shifted = grad * gain.astype(jnp.float32)
    gain_grad = jnp.sum(grad * scaled, axis=0)
    inner = (
        shifted
        - jnp.mean(shifted, axis=-1, keepdims=True)
        - scaled * jnp.mean(shifted * scaled, axis=-1, keepdims=True)
    )
    return (inner * inverse, gain_grad)


def gelu_parts(value):
    normal_cdf = 0.5 * (1.0 + lax.erf(value * (1.0 / math.sqrt(2.0))))
    slope = normal_cdf + value * jnp.exp(-0.5 * value * value) * (1.0 / math.sqrt(2.0 * math.pi))
    return value * normal_cdf, slope


def split_heads(joined, images, length):
    heads = joined.shape[1] // (3 * HEAD_DIM)
    parts = joined.reshape(images, length, 3, heads, HEAD_DIM)
    return (parts[:, :, 0], parts[:, :, 1], parts[:, :, 2])


X, CORES = 4, 2
SLOTS = 32


def x_shift(block, step):
    return lax.ppermute(block, "x", [(i, (i + step) % X) for i in range(X)])


def core_swap(block):
    return lax.ppermute(block, "core", [(0, 1), (1, 0)])


def after(block, earlier):
    return jnp.where(earlier == earlier, block, jnp.zeros_like(block))


def mark(*blocks):
    return sum(block[(0,) * block.ndim].astype(jnp.float32) for block in blocks)


def place(spots, sources, shapes, moves):
    kind = sources[0].dtype
    blocks = [(n, k) for n, source in enumerate(sources) for k in range(source.shape[0])]
    count = sum(len(listed) for listed in moves([0] * spots.shape[0]))
    staged = 2 * sum(math.prod(source.shape) for source in sources)

    def kernel(spots_ref, *refs):
        ins, refs = refs[: len(sources)], refs[len(sources) :]
        outs, refs = refs[: len(shapes)], refs[len(shapes) :]
        stages, (in_sems, out_sems) = refs[: len(sources)], refs[len(sources) :]
        loads = [
            pltpu.make_async_copy(ins[n].at[k], stages[n].at[k], in_sems.at[at])
            for at, (n, k) in enumerate(blocks)
        ]
        for load in loads:
            load.start()
        stores = []
        listed = moves([spots_ref[k] for k in range(spots.shape[0])])
        for load, (n, k), targets in zip(loads, blocks, listed):
            load.wait()
            for cut, at, spot in targets:
                store = pltpu.make_async_copy(
                    stages[n].at[(k,) + cut], outs[at].at[spot], out_sems.at[len(stores)]
                )
                store.start()
                stores.append(store)
        for store in stores:
            store.wait()

    return pl.pallas_call(
        kernel,
        out_shape=[jax.ShapeDtypeStruct(shape, kind) for shape in shapes],
        in_specs=[pl.BlockSpec(memory_space=pltpu.SMEM)]
        + [pl.BlockSpec(memory_space=pl.ANY)] * len(sources),
        out_specs=[pl.BlockSpec(memory_space=pl.ANY)] * len(shapes),
        scratch_shapes=[pltpu.VMEM(source.shape, kind) for source in sources]
        + [pltpu.SemaphoreType.DMA((len(blocks),)), pltpu.SemaphoreType.DMA((count,))],
        compiler_params=pltpu.CompilerParams(vmem_limit_bytes=staged + (2 << 20)),
        cost_estimate=pl.CostEstimate(flops=0, bytes_accessed=2 * staged, transcendentals=0),
    )(spots, *sources)


def gather_pieces(shard):
    return [shard] + [x_shift(shard, step) for step in range(1, X)]


def both_cores(pieces, shapes, targets):
    xi, ci = lax.axis_index("x"), lax.axis_index("core")
    own = jnp.stack(pieces)
    spots = [((xi - k) % X) * CORES + (ci if mine else 1 - ci) for mine in (1, 0) for k in range(X)]
    return place(
        jnp.stack(spots).astype(jnp.int32),
        [own, core_swap(own)],
        shapes,
        lambda spots: [targets(spot) for spot in spots],
    )


def split_rows(left):
    xi, ci = lax.axis_index("x"), lax.axis_index("core")
    rows, wide = left.shape
    blocks = left.T.reshape(X, CORES, wide // (X * CORES), rows)
    blocks = lax.dynamic_slice_in_dim(jnp.concatenate([blocks, blocks], axis=0), xi, X, axis=0)
    own = lax.dynamic_index_in_dim(blocks, ci, 1, keepdims=False)
    other = lax.dynamic_index_in_dim(blocks, 1 - ci, 1, keepdims=False)
    return own.reshape(wide // CORES, rows), other.reshape(wide // CORES, rows)


def scatter_halves(own, other, before=None):
    block = own[0].shape[0] // X
    starts = [sum(part.shape[1] for part in own[:k]) for k in range(len(own))]
    got = core_swap(jnp.concatenate([part.astype(jnp.bfloat16) for part in other], axis=1))
    totals = [
        part + got[:, start : start + part.shape[1]].astype(jnp.float32)
        for part, start in zip(own, starts)
    ]
    low = jnp.concatenate([t[block:].astype(jnp.bfloat16) for t in totals], axis=1)
    if before is not None:
        low = after(low, before)
    arrived = [x_shift(low[(k - 1) * block : k * block], k) for k in range(1, X)]
    sums = []
    for t, start in zip(totals, starts):
        cut = slice(start, start + t.shape[1])
        sums.append(t[:block] + sum(a[:, cut].astype(jnp.float32) for a in arrived))
    return sums, mark(*arrived)


def scatter_dense(up, down):
    (up_own, up_other), (down_own, down_other) = up, down
    width = down_own.shape[1]
    depth, deep = up_own.shape[0] // X, down_own.shape[0] // X
    stripes = up_own.shape[1] // width
    up_total = up_own + core_swap(up_other.astype(jnp.bfloat16)).astype(jnp.float32)
    down_total = down_own + core_swap(down_other.astype(jnp.bfloat16)).astype(jnp.float32)
    arrived = []
    for k in range(1, X):
        up_low = up_total[k * depth : (k + 1) * depth].astype(jnp.bfloat16)
        down_low = down_total[k * deep : (k + 1) * deep].astype(jnp.bfloat16)
        pack = [up_low[:, n * width : (n + 1) * width] for n in range(stripes)] + [down_low]
        arrived.append(x_shift(jnp.concatenate(pack, axis=0), k))
    total = sum(a.astype(jnp.float32) for a in arrived)
    up_sum = up_total[:depth] + jnp.concatenate(
        [total[n * depth : (n + 1) * depth] for n in range(stripes)], axis=1
    )
    return up_sum, down_total[:deep] + total[stripes * depth :], mark(*arrived)


def weight_grad(left, right):
    own, other = split_rows(left)
    return product(own, right), product(other, right)


def attend_forward(stream, gain, in_proj, out_proj, images, length):
    rows, width = stream.shape
    scale = HEAD_DIM ** (-0.5)
    normed_f, saved = norm_rows(stream, gain)
    normed = normed_f.astype(jnp.bfloat16)
    joined = product(normed, in_proj).astype(jnp.bfloat16)
    query, key, value = split_heads(joined, images, length)
    scores = jnp.einsum("sqhd,skhd->shqk", query, key, preferred_element_type=jnp.float32) * scale
    top = jnp.max(scores, axis=-1, keepdims=True)
    expo = jnp.exp(scores - top)
    total = jnp.sum(expo, axis=-1, keepdims=True)
    weights = expo / total
    log_total = top + jnp.log(total)
    mixed = jnp.einsum(
        "shqk,skhd->sqhd", weights.astype(jnp.bfloat16), value, preferred_element_type=jnp.float32
    )
    mixed = mixed.reshape(rows, width).astype(jnp.bfloat16)
    return (stream + product(mixed, out_proj), (normed, saved, joined, log_total, mixed))


def attend_backward(grad, gain, in_proj, out_proj, kept, images, length):
    normed, saved, joined, log_total, mixed = kept
    rows, width = grad.shape
    scale = HEAD_DIM ** (-0.5)
    grad_low = grad.astype(jnp.bfloat16)
    out_grad_w = weight_grad(mixed, grad_low)
    query, key, value = split_heads(joined, images, length)
    mixed_grad = product_bt(grad_low, out_proj).astype(jnp.bfloat16).reshape(query.shape)
    scores = jnp.einsum("sqhd,skhd->shqk", query, key, preferred_element_type=jnp.float32) * scale
    weights = jnp.exp(scores - log_total)
    weight_grad_ = jnp.einsum(
        "sqhd,skhd->shqk", mixed_grad, value, preferred_element_type=jnp.float32
    )
    value_grad = jnp.einsum(
        "shqk,sqhd->skhd",
        weights.astype(jnp.bfloat16),
        mixed_grad,
        preferred_element_type=jnp.float32,
    )
    score_grad = weights * (weight_grad_ - jnp.sum(weights * weight_grad_, axis=-1, keepdims=True))
    score_grad = score_grad.astype(jnp.bfloat16)
    query_grad = (
        jnp.einsum("shqk,skhd->sqhd", score_grad, key, preferred_element_type=jnp.float32) * scale
    )
    key_grad = (
        jnp.einsum("shqk,sqhd->skhd", score_grad, query, preferred_element_type=jnp.float32) * scale
    )
    joined_grad = (
        jnp.stack([query_grad, key_grad, value_grad], axis=2)
        .reshape(rows, 3 * width)
        .astype(jnp.bfloat16)
    )
    in_grad_w = weight_grad(normed, joined_grad)
    stream_grad, gain_grad = norm_back(product_bt(joined_grad, in_proj), gain, saved)
    return (grad + stream_grad, (gain_grad, in_grad_w, out_grad_w))


def dense_forward(stream, gain, up_w, down_w):
    normed_f, saved = norm_rows(stream, gain)
    normed = normed_f.astype(jnp.bfloat16)
    hidden, slope = gelu_parts(product(normed, up_w))
    hidden = hidden.astype(jnp.bfloat16)
    return (stream + product(hidden, down_w), (normed, saved, slope, hidden))


def dense_backward(grad, gain, up_w, down_w, kept):
    normed, saved, slope, hidden = kept
    grad_low = grad.astype(jnp.bfloat16)
    down_grad = weight_grad(hidden, grad_low)
    pre_grad = (product_bt(grad_low, down_w) * slope).astype(jnp.bfloat16)
    up_grad = weight_grad(normed, pre_grad)
    stream_grad, gain_grad = norm_back(product_bt(pre_grad, up_w), gain, saved)
    return (grad + stream_grad, (gain_grad, up_grad, down_grad))


def moe(stream, grad_low, gain, router, up_half, down_half, ready, routes, slot_index, keep_mask):
    rows, width = stream.shape
    experts = router.shape[1]
    slots = experts * SLOTS
    hidden_local = up_half.shape[1] // X
    grad = grad_low.astype(jnp.float32)
    half = width // 2
    normed_f, saved = norm_rows(stream, gain)
    normed = normed_f.astype(jnp.bfloat16)
    logits = product(normed, router)
    top = jnp.max(logits, axis=-1, keepdims=True)
    expo = jnp.exp(logits - top)
    probs = expo / jnp.sum(expo, axis=-1, keepdims=True)
    expert_ids = lax.broadcasted_iota(jnp.int32, (rows, experts), 1)
    keep_float = keep_mask.astype(jnp.float32)
    keep_first, keep_second = keep_float[:, 0:1], keep_float[:, 1:2]
    hot_first = (expert_ids == routes[:, 0:1]).astype(jnp.float32)
    hot_second = (expert_ids == routes[:, 1:2]).astype(jnp.float32)
    gate_first = jnp.sum(probs * hot_first, axis=-1, keepdims=True) * keep_first
    gate_second = jnp.sum(probs * hot_second, axis=-1, keepdims=True) * keep_second
    columns = lax.broadcasted_iota(jnp.int32, (rows, slots), 1)
    target = routes * SLOTS + slot_index
    pick_first = (columns == target[:, 0:1]).astype(jnp.float32) * keep_first
    pick_second = (columns == target[:, 1:2]).astype(jnp.float32) * keep_second
    select = (pick_first + pick_second).astype(jnp.bfloat16)
    slot_gate = jnp.sum(pick_first * gate_first + pick_second * gate_second, axis=0)
    send_rows = product_t(select, normed).astype(jnp.bfloat16)
    send_grad = (product_t(select, grad_low) * slot_gate[:, None]).astype(jnp.bfloat16)
    send = jnp.concatenate(
        [send_rows.reshape(experts, SLOTS, width), send_grad.reshape(experts, SLOTS, width)], axis=1
    )
    send = after(send, ready)
    received = lax.all_to_all(send, ("z", "y"), split_axis=0, concat_axis=0, tiled=True)
    partner = core_swap(received)

    flat = jnp.concatenate([received[:, :SLOTS], partner[:, :SLOTS]], axis=0).reshape(-1, width)
    flat_grad = jnp.concatenate([received[:, SLOTS:], partner[:, SLOTS:]], axis=0).reshape(-1, width)
    hidden, slope = gelu_parts(product(flat, up_half))
    hidden = hidden.astype(jnp.bfloat16)
    partial_out = product(hidden, down_half)
    got_out = core_swap(partial_out[slots:].astype(jnp.bfloat16))
    pre_grad = (product_bt(flat_grad, down_half) * slope).astype(jnp.bfloat16)
    partial_in = product_bt(pre_grad, up_half)
    got_in = core_swap(partial_in[slots:].astype(jnp.bfloat16))
    result = (partial_out[:slots] + got_out.astype(jnp.float32)).astype(jnp.bfloat16)
    in_grad = (partial_in[:slots] + got_in.astype(jnp.float32)).astype(jnp.bfloat16)
    back = jnp.concatenate(
        [result.reshape(experts, SLOTS, width), in_grad.reshape(experts, SLOTS, width)], axis=1
    )
    returned = lax.all_to_all(back, ("z", "y"), split_axis=0, concat_axis=0, tiled=True)
    result_rows = returned[:, :SLOTS].reshape(slots, width)
    back_rows = returned[:, SLOTS:].reshape(slots, width)

    cuts = [slice(k * hidden_local, (k + 1) * hidden_local) for k in range(X)]
    up_parts = [product_t(flat, pre_grad[:, cut]) for cut in cuts]
    down_parts = [product_t(hidden[:, cut], flat_grad) for cut in cuts]
    arrived = []
    for k in range(1, X):
        low_up = up_parts[k].astype(jnp.bfloat16)
        pack = jnp.concatenate(
            [low_up[:half], low_up[half:], down_parts[k].astype(jnp.bfloat16)], axis=1
        )
        arrived.append(x_shift(pack, -k))
    total = sum(a.astype(jnp.float32) for a in arrived)
    up_grad = up_parts[0] + jnp.concatenate(
        [total[:, :hidden_local], total[:, hidden_local : 2 * hidden_local]], axis=0
    )
    down_grad = down_parts[0] + total[:, 2 * hidden_local :]
    sent = mark(*arrived)

    first = product(pick_first.astype(jnp.bfloat16), result_rows)
    second = product(pick_second.astype(jnp.bfloat16), result_rows)
    new_stream = stream + gate_first * first + gate_second * second
    gate_grad_first = jnp.sum(grad * first, axis=-1, keepdims=True) * keep_first
    gate_grad_second = jnp.sum(grad * second, axis=-1, keepdims=True) * keep_second
    probs_grad = gate_grad_first * hot_first + gate_grad_second * hot_second
    logit_grad = probs * (probs_grad - jnp.sum(probs * probs_grad, axis=-1, keepdims=True))
    logit_grad = logit_grad.astype(jnp.bfloat16)
    router_grad = product_t(normed, logit_grad)
    normed_grad = product_bt(logit_grad, router) + product(select, back_rows)
    stream_grad, gain_grad = norm_back(normed_grad, gain, saved)
    return (new_stream, grad + stream_grad, (gain_grad, router_grad, up_grad, down_grad), sent)


def shards(
    tokens,
    norm_attn_a,
    in_proj_a,
    out_proj_a,
    norm_dense,
    dense_up,
    dense_down,
    norm_attn_b,
    in_proj_b,
    out_proj_b,
    norm_moe,
    router,
    expert_up,
    expert_down,
    routes,
    slot_index,
    keep_mask,
    output_grad,
):
    images, length, width = tokens.shape
    rows = images * length
    stream = tokens.reshape(rows, width).astype(jnp.float32)
    flat_routes = routes.reshape(rows, 2)
    flat_slots = slot_index.reshape(rows, 2)
    flat_keep = keep_mask.reshape(rows, 2)
    experts = router.shape[1]
    small = jnp.concatenate(
        [
            jnp.stack([norm_attn_a, norm_dense, norm_attn_b, norm_moe], axis=1),
            router,
            jnp.zeros((router.shape[0], 128 - 4 - experts), router.dtype),
        ],
        axis=1,
    )
    wide_in, wide_out = in_proj_a.shape[1], out_proj_a.shape[1]
    blocks, depth = X * CORES, in_proj_a.shape[0]
    every = slice(None)

    def side_by_side(widths):
        starts = [sum(widths[:at]) for at in range(len(widths))]
        return lambda spot: [
            ((every, pl.ds(start, wide)), at, (spot,))
            for at, (start, wide) in enumerate(zip(starts, widths))
        ]

    pieces = gather_pieces(jnp.concatenate([in_proj_a, out_proj_a, small], axis=1))
    reached = mark(*pieces[1:])
    widths = [wide_in, wide_out, 128]
    in_aa, out_aa, small_all = both_cores(
        pieces, [(blocks, depth, wide) for wide in widths], side_by_side(widths)
    )
    in_aa, out_aa, small_all = (w.reshape(width, -1) for w in (in_aa, out_aa, small_all))
    gain_aa, gain_dd, gain_bb, gain_mm = (small_all[:, k] for k in range(4))
    router_full = small_all[:, 4 : 4 + experts]

    stripes = dense_up.shape[1] // width
    high = stripes * depth
    pieces = gather_pieces(
        after(
            jnp.concatenate(
                [dense_up[:, k * width : (k + 1) * width] for k in range(stripes)] + [dense_down], axis=0
            ),
            reached,
        )
    )
    reached = mark(*pieces[1:])
    (up_dd,) = both_cores(
        [piece[:high] for piece in pieces],
        [(blocks, depth, stripes * width)],
        lambda spot: [
            ((pl.ds(k * depth, depth), every), 0, (spot, every, pl.ds(k * width, width)))
            for k in range(stripes)
        ],
    )
    (down_dd,) = both_cores(
        [piece[high:] for piece in pieces],
        [(blocks, dense_down.shape[0], width)],
        lambda spot: [((every, every), 0, (spot,))],
    )
    up_dd, down_dd = up_dd.reshape(width, -1), down_dd.reshape(-1, width)

    pieces = gather_pieces(after(jnp.concatenate([in_proj_b, out_proj_b], axis=1), reached))
    widths = [wide_in, wide_out]
    in_bb, out_bb = both_cores(
        pieces, [(blocks, depth, wide) for wide in widths], side_by_side(widths)
    )
    in_bb, out_bb = in_bb.reshape(width, -1), out_bb.reshape(width, -1)

    up_local, down_local = expert_up[0], expert_down[0]
    half, units = width // 2, up_local.shape[1]
    packs = gather_pieces(
        after(jnp.concatenate([up_local[:half], up_local[half:], down_local], axis=1), reached)
    )

    def unpack(k):
        parts = [
            ((every, pl.ds(part * units, units)), 0, (pl.ds(part * half, half), pl.ds(k * units, units)))
            for part in range(2)
        ]
        return parts + [((every, pl.ds(2 * units, width)), 1, (pl.ds(k * units, units),))]

    up_half, down_half = place(
        jnp.zeros((1,), jnp.int32),
        [pack[None] for pack in packs],
        [(width, X * units), (X * units, width)],
        lambda _: [unpack(k) for k in range(X)],
    )

    stream_one, kept_one = attend_forward(stream, gain_aa, in_aa, out_aa, images, length)
    stream_two, kept_two = dense_forward(stream_one, gain_dd, up_dd, down_dd)
    stream_three, kept_three = attend_forward(stream_two, gain_bb, in_bb, out_bb, images, length)
    stream_four, grad, moe_grads, sent = moe(
        stream_three,
        output_grad.reshape(rows, width),
        gain_mm,
        router_full,
        up_half,
        down_half,
        mark(*packs[1:]),
        flat_routes,
        flat_slots,
        flat_keep,
    )
    output = stream_four.astype(jnp.bfloat16).reshape(images, length, width)
    grad, attn_b_grads = attend_backward(grad, gain_bb, in_bb, out_bb, kept_three, images, length)
    (in_b, out_b), sent_b = scatter_halves(*zip(attn_b_grads[1], attn_b_grads[2]))
    grad = after(grad, sent)
    grad, dense_grads = dense_backward(grad, gain_dd, up_dd, down_dd, kept_two)
    up, down, sent_d = scatter_dense(dense_grads[1], dense_grads[2])
    grad = after(grad, sent_b)
    grad, attn_a_grads = attend_backward(grad, gain_aa, in_aa, out_aa, kept_one, images, length)
    input_grad = grad.reshape(images, length, width)
    small_grad = jnp.concatenate(
        [
            jnp.stack([attn_a_grads[0], dense_grads[0], attn_b_grads[0], moe_grads[0]], axis=0),
            moe_grads[1].T,
            jnp.zeros((128 - 4 - experts, width), jnp.float32),
        ],
        axis=0,
    )
    (in_a, out_a, small_share), _ = scatter_halves(
        *zip(attn_a_grads[1], attn_a_grads[2], split_rows(small_grad)), before=sent_d
    )
    shares = [in_a, jnp.concatenate([out_a, small_share], axis=1), up, down, in_b, out_b]
    totals = lax.psum([share.astype(jnp.bfloat16) for share in shares], ("z", "y"))
    in_a, out_a, up, down, in_b, out_b = [t.astype(jnp.float32) for t in totals]
    out_a, small_total = out_a[:, :wide_out], out_a[:, wide_out:]
    return (
        output,
        input_grad,
        small_total[:, 0],
        in_a,
        out_a,
        small_total[:, 1],
        up,
        down,
        small_total[:, 2],
        in_b,
        out_b,
        small_total[:, 3],
        small_total[:, 4 : 4 + experts],
        moe_grads[2][None],
        moe_grads[3][None],
    )


def solution(mesh):
    places = Mesh(mesh.devices.reshape(X, CORES, 4, 4), ("x", "core", "z", "y"))
    dp, expert = ("x", "core"), ("z", "y")
    images = P(dp + expert, None, None)
    return jax.shard_map(
        shards,
        mesh=places,
        in_specs=(
            images,
            P(dp),
            P(dp, None),
            P(dp, None),
            P(dp),
            P(dp, None),
            P(dp, None),
            P(dp),
            P(dp, None),
            P(dp, None),
            P(dp),
            P(dp, None),
            P(expert, None, dp),
            P(expert, dp, None),
            images,
            images,
            images,
            images,
        ),
        out_specs=(
            images,
            images,
            P(dp),
            P(dp, None),
            P(dp, None),
            P(dp),
            P(dp, None),
            P(dp, None),
            P(dp),
            P(dp, None),
            P(dp, None),
            P(dp),
            P(dp, None),
            P(expert, None, dp),
            P(expert, dp, None),
        ),
        check_vma=False,
    )
```

```python
import math

import jax
import jax.numpy as jnp
from jax import lax
from jax.experimental import pallas as pl
from jax.experimental.pallas import tpu as pltpu
from jax.sharding import Mesh, PartitionSpec as P

HEAD_DIM = 64


epsilon = 1e-06


def product(left, right):
    return jnp.dot(left, right, preferred_element_type=jnp.float32)


def product_t(left, right):
    return lax.dot_general(
        left, right, (((0,), (0,)), ((), ())), preferred_element_type=jnp.float32
    )


def product_bt(left, right):
    return lax.dot_general(
        left, right, (((1,), (1,)), ((), ())), preferred_element_type=jnp.float32
    )


def norm_rows(stream, gain):
    center = jnp.mean(stream, axis=-1, keepdims=True)
    centred = stream - center
    spread = jnp.mean(centred * centred, axis=-1, keepdims=True)
    inverse = lax.rsqrt(spread + epsilon)
    scaled = centred * inverse
    return (scaled * gain.astype(jnp.float32), (scaled, inverse))


def norm_back(grad, gain, saved):
    scaled, inverse = saved
    shifted = grad * gain.astype(jnp.float32)
    gain_grad = jnp.sum(grad * scaled, axis=0)
    inner = (
        shifted
        - jnp.mean(shifted, axis=-1, keepdims=True)
        - scaled * jnp.mean(shifted * scaled, axis=-1, keepdims=True)
    )
    return (inner * inverse, gain_grad)


def gelu_parts(value):
    normal_cdf = 0.5 * (1.0 + lax.erf(value * (1.0 / math.sqrt(2.0))))
    slope = normal_cdf + value * jnp.exp(-0.5 * value * value) * (1.0 / math.sqrt(2.0 * math.pi))
    return value * normal_cdf, slope


def split_heads(joined, images, length):
    heads = joined.shape[1] // (3 * HEAD_DIM)
    parts = joined.reshape(images, length, 3, heads, HEAD_DIM)
    return (parts[:, :, 0], parts[:, :, 1], parts[:, :, 2])


X, CORES = 4, 2
SLOTS = 32


def shift(block, axis, step):
    return lax.ppermute(block, axis, [(i, (i + step) % X) for i in range(X)])


def x_shift(block, step):
    return shift(block, "x", step)


def rolled(array, start, axis):
    doubled = jnp.concatenate([array, array], axis=axis)
    return lax.dynamic_slice_in_dim(doubled, start, X, axis=axis)


def core_swap(block):
    return lax.ppermute(block, "core", [(0, 1), (1, 0)])


def place(spots, sources, shapes, moves, count):
    kind = sources[0].dtype
    blocks = [(n, k) for n, source in enumerate(sources) for k in range(source.shape[0])]
    staged = 2 * sum(math.prod(source.shape) for source in sources)

    def kernel(spots_ref, *refs):
        ins, refs = refs[: len(sources)], refs[len(sources) :]
        outs, refs = refs[: len(shapes)], refs[len(shapes) :]
        stages, (in_sems, out_sems) = refs[: len(sources)], refs[len(sources) :]
        loads = [
            pltpu.make_async_copy(ins[n].at[k], stages[n].at[k], in_sems.at[at])
            for at, (n, k) in enumerate(blocks)
        ]
        for load in loads:
            load.start()
        stores = []
        listed = moves([spots_ref[k] for k in range(spots.shape[0])])
        for load, (n, k), targets in zip(loads, blocks, listed):
            load.wait()
            for cut, at, spot in targets:
                store = pltpu.make_async_copy(
                    stages[n].at[(k,) + cut], outs[at].at[spot], out_sems.at[len(stores)]
                )
                store.start()
                stores.append(store)
        for store in stores:
            store.wait()

    return pl.pallas_call(
        kernel,
        out_shape=[jax.ShapeDtypeStruct(shape, kind) for shape in shapes],
        in_specs=[pl.BlockSpec(memory_space=pltpu.SMEM)]
        + [pl.BlockSpec(memory_space=pl.ANY)] * len(sources),
        out_specs=[pl.BlockSpec(memory_space=pl.ANY)] * len(shapes),
        scratch_shapes=[pltpu.VMEM(source.shape, kind) for source in sources]
        + [pltpu.SemaphoreType.DMA((len(blocks),)), pltpu.SemaphoreType.DMA((count,))],
        compiler_params=pltpu.CompilerParams(vmem_limit_bytes=staged + (2 << 20)),
        cost_estimate=pl.CostEstimate(flops=0, bytes_accessed=2 * staged, transcendentals=0),
    )(spots, *sources)


def gather_pieces(shard):
    return [shard] + [x_shift(shard, step) for step in range(1, X)]


def both_cores(pieces, shapes, targets, each):
    xi, ci = lax.axis_index("x"), lax.axis_index("core")
    own = jnp.stack(pieces)
    spots = [((xi - k) % X) * CORES + (ci if mine else 1 - ci) for mine in (1, 0) for k in range(X)]
    return place(
        jnp.stack(spots).astype(jnp.int32),
        [own, core_swap(own)],
        shapes,
        lambda spots: [targets(spot) for spot in spots],
        CORES * X * each,
    )


def gather_dense(up_shard, down_shard):
    xi, ci, zi, yi = (lax.axis_index(name) for name in ("x", "core", "z", "y"))
    depth, width = up_shard.shape[0], down_shard.shape[1]
    up_part = lax.dynamic_slice_in_dim(up_shard, zi * width, width, axis=1)
    down_part = lax.dynamic_slice_in_dim(down_shard, yi * depth, depth, axis=0)
    pieces = gather_pieces(jnp.concatenate([up_part, down_part], axis=0))
    up_x = jnp.stack([piece[:depth] for piece in pieces])
    down_x = jnp.stack([piece[depth:] for piece in pieces])
    up_own = lax.all_gather(up_x, "z", axis=0, tiled=True)
    down_own = lax.all_gather(down_x, "y", axis=0, tiled=True)
    rows = [
        ((xi - k) % X) * CORES + (ci if mine else 1 - ci)
        for mine in (1, 0)
        for _ in range(X)
        for k in range(X)
    ]
    every = slice(None)
    count = CORES * X * X
    parts = [n // X % X for n in range(count)]

    def columns(spots):
        return [
            [((every, every), 0, (spots[n], every, pl.ds(parts[n] * width, width)))]
            for n in range(count)
        ]

    def stripes(spots):
        return [[((every, every), 0, (spots[n], parts[n]))] for n in range(count)]

    rows = jnp.stack(rows).astype(jnp.int32)
    (up,) = place(
        rows, [up_own, core_swap(up_own)], [(X * CORES, depth, X * width)], columns, count
    )
    (down,) = place(
        rows, [down_own, core_swap(down_own)], [(X * CORES, X, depth, width)], stripes, count
    )
    return up.reshape(-1, X * width), down.reshape(-1, width)


def split_rows(left):
    xi, ci = lax.axis_index("x"), lax.axis_index("core")
    rows, wide = left.shape
    blocks = left.T.reshape(X, CORES, wide // (X * CORES), rows)
    blocks = lax.dynamic_slice_in_dim(jnp.concatenate([blocks, blocks], axis=0), xi, X, axis=0)
    own = lax.dynamic_index_in_dim(blocks, ci, 1, keepdims=False)
    other = lax.dynamic_index_in_dim(blocks, 1 - ci, 1, keepdims=False)
    return own.reshape(wide // CORES, rows), other.reshape(wide // CORES, rows)


def scatter_halves(own, other):
    block = own[0].shape[0] // X
    starts = [sum(part.shape[1] for part in own[:k]) for k in range(len(own))]
    got = core_swap(jnp.concatenate([part.astype(jnp.bfloat16) for part in other], axis=1))
    totals = [
        part + got[:, start : start + part.shape[1]].astype(jnp.float32)
        for part, start in zip(own, starts)
    ]
    low = jnp.concatenate([t[block:].astype(jnp.bfloat16) for t in totals], axis=1)
    arrived = [x_shift(low[(k - 1) * block : k * block], k) for k in range(1, X)]
    sums = []
    for t, start in zip(totals, starts):
        cut = slice(start, start + t.shape[1])
        sums.append(t[:block] + sum(a[:, cut].astype(jnp.float32) for a in arrived))
    return sums


def scatter_whole(part):
    return lax.psum_scatter(
        part.astype(jnp.bfloat16), ("x", "core"), scatter_dimension=0, tiled=True
    )


def sum_over_zy(shares, small):
    spots, wide = 16, 768
    parts = []
    for share in shares:
        low = share.astype(jnp.bfloat16)
        stripes = [low[:, k : k + wide] for k in range(0, low.shape[1], wide)]
        parts.append(jnp.concatenate(stripes, axis=0).reshape(spots, -1, wide))
    if small is not None:
        last = small.astype(jnp.bfloat16).reshape(spots, -1, wide)
        parts.append(jnp.pad(last, ((0, 0), (0, 8 - last.shape[1]), (0, 0))))
    packed = jnp.concatenate(parts, axis=1)
    came = lax.all_to_all(packed, ("z", "y"), split_axis=0, concat_axis=0, tiled=True)
    mine = jnp.sum(came.astype(jnp.float32), axis=0).astype(jnp.bfloat16)
    copies = jnp.broadcast_to(mine[None], packed.shape)
    back = lax.all_to_all(copies, ("z", "y"), split_axis=0, concat_axis=0, tiled=True)
    sums, start = [], 0
    for share, part in zip(shares, parts):
        depth, high = share.shape[0], part.shape[1]
        rows = back[:, start : start + high].reshape(-1, wide).astype(jnp.float32)
        start += high
        sums.append(
            jnp.concatenate([rows[k : k + depth] for k in range(0, rows.shape[0], depth)], axis=1)
        )
    if small is None:
        return sums
    rest = back[:, start : start + last.shape[1]]
    return sums, rest.reshape(small.shape).astype(jnp.float32)


def weight_grad(left, right):
    own, other = split_rows(left)
    return product(own, right), product(other, right)


def attend_forward(stream, gain, in_proj, out_proj, images, length):
    rows, width = stream.shape
    scale = HEAD_DIM ** (-0.5)
    normed_f, saved = norm_rows(stream, gain)
    normed = normed_f.astype(jnp.bfloat16)
    joined = product(normed, in_proj).astype(jnp.bfloat16)
    query, key, value = split_heads(joined, images, length)
    scores = jnp.einsum("sqhd,skhd->shqk", query, key, preferred_element_type=jnp.float32) * scale
    top = jnp.max(scores, axis=-1, keepdims=True)
    expo = jnp.exp(scores - top)
    total = jnp.sum(expo, axis=-1, keepdims=True)
    weights = expo / total
    log_total = top + jnp.log(total)
    mixed = jnp.einsum(
        "shqk,skhd->sqhd", weights.astype(jnp.bfloat16), value, preferred_element_type=jnp.float32
    )
    mixed = mixed.reshape(rows, width).astype(jnp.bfloat16)
    return (stream + product(mixed, out_proj), (normed, saved, joined, log_total, mixed))


def attend_backward(grad, gain, in_proj, out_proj, kept, images, length, weight_grad):
    normed, saved, joined, log_total, mixed = kept
    rows, width = grad.shape
    scale = HEAD_DIM ** (-0.5)
    grad_low = grad.astype(jnp.bfloat16)
    out_grad_w = weight_grad(mixed, grad_low)
    query, key, value = split_heads(joined, images, length)
    mixed_grad = product_bt(grad_low, out_proj).astype(jnp.bfloat16).reshape(query.shape)
    scores = jnp.einsum("sqhd,skhd->shqk", query, key, preferred_element_type=jnp.float32) * scale
    weights = jnp.exp(scores - log_total)
    weight_grad_ = jnp.einsum(
        "sqhd,skhd->shqk", mixed_grad, value, preferred_element_type=jnp.float32
    )
    value_grad = jnp.einsum(
        "shqk,sqhd->skhd",
        weights.astype(jnp.bfloat16),
        mixed_grad,
        preferred_element_type=jnp.float32,
    )
    score_grad = weights * (weight_grad_ - jnp.sum(weights * weight_grad_, axis=-1, keepdims=True))
    score_grad = score_grad.astype(jnp.bfloat16)
    query_grad = (
        jnp.einsum("shqk,skhd->sqhd", score_grad, key, preferred_element_type=jnp.float32) * scale
    )
    key_grad = (
        jnp.einsum("shqk,sqhd->skhd", score_grad, query, preferred_element_type=jnp.float32) * scale
    )
    joined_grad = (
        jnp.stack([query_grad, key_grad, value_grad], axis=2)
        .reshape(rows, 3 * width)
        .astype(jnp.bfloat16)
    )
    in_grad_w = weight_grad(normed, joined_grad)
    stream_grad, gain_grad = norm_back(product_bt(joined_grad, in_proj), gain, saved)
    return (grad + stream_grad, (gain_grad, in_grad_w, out_grad_w))


def dense_forward(stream, gain, up_w, down_w):
    normed_f, saved = norm_rows(stream, gain)
    normed = normed_f.astype(jnp.bfloat16)
    hidden, slope = gelu_parts(product(normed, up_w))
    hidden = hidden.astype(jnp.bfloat16)
    return (stream + product(hidden, down_w), (normed, saved, slope, hidden))


def dense_backward(grad, gain, up_w, down_w, kept):
    normed, saved, slope, hidden = kept
    grad_low = grad.astype(jnp.bfloat16)
    pre_grad = (product_bt(grad_low, down_w) * slope).astype(jnp.bfloat16)
    up_grad = scatter_whole(product_t(normed, pre_grad))
    down_grad = scatter_whole(product_t(hidden, grad_low))
    stream_grad, gain_grad = norm_back(product_bt(pre_grad, up_w), gain, saved)
    return (grad + stream_grad, (gain_grad, up_grad, down_grad))


def moe(stream, grad_low, gain, router, up_half, down_half, routes, slot_index, keep_mask):
    rows, width = stream.shape
    experts = router.shape[1]
    slots = experts * SLOTS
    grad = grad_low.astype(jnp.float32)
    normed_f, saved = norm_rows(stream, gain)
    normed = normed_f.astype(jnp.bfloat16)
    logits = product(normed, router)
    top = jnp.max(logits, axis=-1, keepdims=True)
    expo = jnp.exp(logits - top)
    probs = expo / jnp.sum(expo, axis=-1, keepdims=True)
    expert_ids = lax.broadcasted_iota(jnp.int32, (rows, experts), 1)
    keep_float = keep_mask.astype(jnp.float32)
    keep_first, keep_second = keep_float[:, 0:1], keep_float[:, 1:2]
    hot_first = (expert_ids == routes[:, 0:1]).astype(jnp.float32)
    hot_second = (expert_ids == routes[:, 1:2]).astype(jnp.float32)
    gate_first = jnp.sum(probs * hot_first, axis=-1, keepdims=True) * keep_first
    gate_second = jnp.sum(probs * hot_second, axis=-1, keepdims=True) * keep_second
    columns = lax.broadcasted_iota(jnp.int32, (rows, slots), 1)
    target = routes * SLOTS + slot_index
    pick_first = (columns == target[:, 0:1]).astype(jnp.float32) * keep_first
    pick_second = (columns == target[:, 1:2]).astype(jnp.float32) * keep_second
    select = (pick_first + pick_second).astype(jnp.bfloat16)
    slot_gate = jnp.sum(pick_first * gate_first + pick_second * gate_second, axis=0)
    send_rows = product_t(select, normed).astype(jnp.bfloat16)
    send_grad = (product_t(select, grad_low) * slot_gate[:, None]).astype(jnp.bfloat16)
    send = jnp.concatenate(
        [send_rows.reshape(experts, SLOTS, width), send_grad.reshape(experts, SLOTS, width)], axis=1
    )
    received = lax.all_to_all(send, ("z", "y"), split_axis=0, concat_axis=0, tiled=True)
    partner = core_swap(received)

    flat = jnp.concatenate([received[:, :SLOTS], partner[:, :SLOTS]], axis=0).reshape(-1, width)
    flat_grad = jnp.concatenate([received[:, SLOTS:], partner[:, SLOTS:]], axis=0).reshape(-1, width)
    hidden, slope = gelu_parts(product_bt(flat, up_half))
    hidden = hidden.astype(jnp.bfloat16)
    partial_out = product(hidden, down_half)
    got_out = core_swap(partial_out[slots:].astype(jnp.bfloat16))
    pre_grad = (product_bt(flat_grad, down_half) * slope).astype(jnp.bfloat16)
    partial_in = product(pre_grad, up_half)
    got_in = core_swap(partial_in[slots:].astype(jnp.bfloat16))
    result = (partial_out[:slots] + got_out.astype(jnp.float32)).astype(jnp.bfloat16)
    in_grad = (partial_in[:slots] + got_in.astype(jnp.float32)).astype(jnp.bfloat16)
    back = jnp.concatenate(
        [result.reshape(experts, SLOTS, width), in_grad.reshape(experts, SLOTS, width)], axis=1
    )
    returned = lax.all_to_all(back, ("z", "y"), split_axis=0, concat_axis=0, tiled=True)
    result_rows = returned[:, :SLOTS].reshape(slots, width)
    back_rows = returned[:, SLOTS:].reshape(slots, width)

    down_grad = lax.psum_scatter(
        product_t(hidden, flat_grad).astype(jnp.bfloat16), "x", scatter_dimension=0, tiled=True
    ).astype(jnp.float32)
    up_grad = lax.psum_scatter(
        product_t(pre_grad, flat).astype(jnp.bfloat16), "x", scatter_dimension=0, tiled=True
    )
    up_grad = up_grad.astype(jnp.float32).T

    first = product(pick_first.astype(jnp.bfloat16), result_rows)
    second = product(pick_second.astype(jnp.bfloat16), result_rows)
    new_stream = stream + gate_first * first + gate_second * second
    gate_grad_first = jnp.sum(grad * first, axis=-1, keepdims=True) * keep_first
    gate_grad_second = jnp.sum(grad * second, axis=-1, keepdims=True) * keep_second
    probs_grad = gate_grad_first * hot_first + gate_grad_second * hot_second
    logit_grad = probs * (probs_grad - jnp.sum(probs * probs_grad, axis=-1, keepdims=True))
    logit_grad = logit_grad.astype(jnp.bfloat16)
    router_grad = product_t(normed, logit_grad)
    normed_grad = product_bt(logit_grad, router) + product(select, back_rows)
    stream_grad, gain_grad = norm_back(normed_grad, gain, saved)
    return (new_stream, grad + stream_grad, (gain_grad, router_grad, up_grad, down_grad))


def shards(
    tokens,
    norm_attn_a,
    in_proj_a,
    out_proj_a,
    norm_dense,
    dense_up,
    dense_down,
    norm_attn_b,
    in_proj_b,
    out_proj_b,
    norm_moe,
    router,
    expert_up,
    expert_down,
    routes,
    slot_index,
    keep_mask,
    output_grad,
):
    images, length, width = tokens.shape
    rows = images * length
    stream = tokens.reshape(rows, width).astype(jnp.float32)
    flat_routes = routes.reshape(rows, 2)
    flat_slots = slot_index.reshape(rows, 2)
    flat_keep = keep_mask.reshape(rows, 2)
    experts = router.shape[1]
    small = jnp.concatenate(
        [
            jnp.stack([norm_attn_a, norm_dense, norm_attn_b, norm_moe], axis=1),
            router,
            jnp.zeros((router.shape[0], 128 - 4 - experts), router.dtype),
        ],
        axis=1,
    )
    wide_in, wide_out = in_proj_a.shape[1], out_proj_a.shape[1]
    blocks, depth = X * CORES, in_proj_a.shape[0]
    every = slice(None)

    def side_by_side(widths):
        starts = [sum(widths[:at]) for at in range(len(widths))]
        return lambda spot: [
            ((every, pl.ds(start, wide)), at, (spot,))
            for at, (start, wide) in enumerate(zip(starts, widths))
        ]

    pieces = gather_pieces(jnp.concatenate([in_proj_a, out_proj_a, small], axis=1))
    widths = [wide_in, wide_out, 128]
    in_aa, out_aa, small_all = both_cores(
        pieces, [(blocks, depth, wide) for wide in widths], side_by_side(widths), len(widths)
    )
    in_aa, out_aa, small_all = (w.reshape(width, -1) for w in (in_aa, out_aa, small_all))
    gain_aa, gain_dd, gain_bb, gain_mm = (small_all[:, k] for k in range(4))
    router_full = small_all[:, 4 : 4 + experts]

    up_dd, down_dd = gather_dense(dense_up, dense_down)

    pieces = gather_pieces(jnp.concatenate([in_proj_b, out_proj_b], axis=1))
    widths = [wide_in, wide_out]
    in_bb, out_bb = both_cores(
        pieces, [(blocks, depth, wide) for wide in widths], side_by_side(widths), len(widths)
    )
    in_bb, out_bb = in_bb.reshape(width, -1), out_bb.reshape(width, -1)

    up_half = lax.all_gather(expert_up[0].T, "x", axis=0, tiled=True)
    down_half = lax.all_gather(expert_down[0], "x", axis=0, tiled=True)

    stream_one, kept_one = attend_forward(stream, gain_aa, in_aa, out_aa, images, length)
    stream_two, kept_two = dense_forward(stream_one, gain_dd, up_dd, down_dd)
    stream_three, kept_three = attend_forward(stream_two, gain_bb, in_bb, out_bb, images, length)
    stream_four, grad, moe_grads = moe(
        stream_three,
        output_grad.reshape(rows, width),
        gain_mm,
        router_full,
        up_half,
        down_half,
        flat_routes,
        flat_slots,
        flat_keep,
    )
    output = stream_four.astype(jnp.bfloat16).reshape(images, length, width)
    grad, attn_b_grads = attend_backward(
        grad, gain_bb, in_bb, out_bb, kept_three, images, length, product_t
    )
    share_b = scatter_whole(jnp.concatenate(attn_b_grads[1:], axis=1))
    grad, dense_grads = dense_backward(grad, gain_dd, up_dd, down_dd, kept_two)
    grad, attn_a_grads = attend_backward(
        grad, gain_aa, in_aa, out_aa, kept_one, images, length, weight_grad
    )
    input_grad = grad.reshape(images, length, width)
    small_grad = jnp.concatenate(
        [
            jnp.stack([attn_a_grads[0], dense_grads[0], attn_b_grads[0], moe_grads[0]], axis=0),
            moe_grads[1].T,
            jnp.zeros((128 - 4 - experts, width), jnp.float32),
        ],
        axis=0,
    )
    in_a, out_a, small_share = scatter_halves(
        *zip(attn_a_grads[1], attn_a_grads[2], split_rows(small_grad))
    )
    share_a = jnp.concatenate([in_a, out_a], axis=1)
    (share_a, share_b), small_total = sum_over_zy([share_a, share_b], small_share)
    up, down = sum_over_zy(dense_grads[1:], None)
    in_a, out_a = share_a[:, :wide_in], share_a[:, wide_in:]
    in_b, out_b = share_b[:, :wide_in], share_b[:, wide_in:]
    return (
        output,
        input_grad,
        small_total[:, 0],
        in_a,
        out_a,
        small_total[:, 1],
        up,
        down,
        small_total[:, 2],
        in_b,
        out_b,
        small_total[:, 3],
        small_total[:, 4 : 4 + experts],
        moe_grads[2][None],
        moe_grads[3][None],
    )


def solution(mesh):
    places = Mesh(mesh.devices.reshape(X, CORES, 4, 4), ("x", "core", "z", "y"))
    dp, expert = ("x", "core"), ("z", "y")
    images = P(dp + expert, None, None)
    return jax.shard_map(
        shards,
        mesh=places,
        in_specs=(
            images,
            P(dp),
            P(dp, None),
            P(dp, None),
            P(dp),
            P(dp, None),
            P(dp, None),
            P(dp),
            P(dp, None),
            P(dp, None),
            P(dp),
            P(dp, None),
            P(expert, None, dp),
            P(expert, dp, None),
            images,
            images,
            images,
            images,
        ),
        out_specs=(
            images,
            images,
            P(dp),
            P(dp, None),
            P(dp, None),
            P(dp),
            P(dp, None),
            P(dp, None),
            P(dp),
            P(dp, None),
            P(dp, None),
            P(dp),
            P(dp, None),
            P(expert, None, dp),
            P(expert, dp, None),
        ),
        check_vma=False,
    )
```

```python
import math

import jax
import jax.numpy as jnp
from jax import lax
from jax.experimental import pallas as pl
from jax.experimental.pallas import tpu as pltpu
from jax.sharding import Mesh, PartitionSpec as P

HEAD_DIM = 64


epsilon = 1e-06


def product(left, right):
    return jnp.dot(left, right, preferred_element_type=jnp.float32)


def product_t(left, right):
    return lax.dot_general(
        left, right, (((0,), (0,)), ((), ())), preferred_element_type=jnp.float32
    )


def product_bt(left, right):
    return lax.dot_general(
        left, right, (((1,), (1,)), ((), ())), preferred_element_type=jnp.float32
    )


def norm_rows(stream, gain):
    center = jnp.mean(stream, axis=-1, keepdims=True)
    centred = stream - center
    spread = jnp.mean(centred * centred, axis=-1, keepdims=True)
    inverse = lax.rsqrt(spread + epsilon)
    scaled = centred * inverse
    return (scaled * gain.astype(jnp.float32), (scaled, inverse))


def norm_back(grad, gain, saved):
    scaled, inverse = saved
    shifted = grad * gain.astype(jnp.float32)
    gain_grad = jnp.sum(grad * scaled, axis=0)
    inner = (
        shifted
        - jnp.mean(shifted, axis=-1, keepdims=True)
        - scaled * jnp.mean(shifted * scaled, axis=-1, keepdims=True)
    )
    return (inner * inverse, gain_grad)


def gelu_parts(value):
    normal_cdf = 0.5 * (1.0 + lax.erf(value * (1.0 / math.sqrt(2.0))))
    slope = normal_cdf + value * jnp.exp(-0.5 * value * value) * (1.0 / math.sqrt(2.0 * math.pi))
    return value * normal_cdf, slope


def split_heads(joined, images, length):
    heads = joined.shape[1] // (3 * HEAD_DIM)
    parts = joined.reshape(images, length, 3, heads, HEAD_DIM)
    return (parts[:, :, 0], parts[:, :, 1], parts[:, :, 2])


X, CORES = 4, 2
SLOTS = 32


def shift(block, axis, step):
    return lax.ppermute(block, axis, [(i, (i + step) % X) for i in range(X)])


def x_shift(block, step):
    return shift(block, "x", step)


def rolled(array, start, axis):
    doubled = jnp.concatenate([array, array], axis=axis)
    return lax.dynamic_slice_in_dim(doubled, start, X, axis=axis)


def core_swap(block):
    return lax.ppermute(block, "core", [(0, 1), (1, 0)])


def after(block, earlier):
    return jnp.where(earlier == earlier, block, jnp.zeros_like(block))


def mark(*blocks):
    return sum(block[(0,) * block.ndim].astype(jnp.float32) for block in blocks)


def place(spots, sources, shapes, moves, count):
    kind = sources[0].dtype
    blocks = [(n, k) for n, source in enumerate(sources) for k in range(source.shape[0])]
    staged = 2 * sum(math.prod(source.shape) for source in sources)

    def kernel(spots_ref, *refs):
        ins, refs = refs[: len(sources)], refs[len(sources) :]
        outs, refs = refs[: len(shapes)], refs[len(shapes) :]
        stages, (in_sems, out_sems) = refs[: len(sources)], refs[len(sources) :]
        loads = [
            pltpu.make_async_copy(ins[n].at[k], stages[n].at[k], in_sems.at[at])
            for at, (n, k) in enumerate(blocks)
        ]
        for load in loads:
            load.start()
        stores = []
        listed = moves([spots_ref[k] for k in range(spots.shape[0])])
        for load, (n, k), targets in zip(loads, blocks, listed):
            load.wait()
            for cut, at, spot in targets:
                store = pltpu.make_async_copy(
                    stages[n].at[(k,) + cut], outs[at].at[spot], out_sems.at[len(stores)]
                )
                store.start()
                stores.append(store)
        for store in stores:
            store.wait()

    return pl.pallas_call(
        kernel,
        out_shape=[jax.ShapeDtypeStruct(shape, kind) for shape in shapes],
        in_specs=[pl.BlockSpec(memory_space=pltpu.SMEM)]
        + [pl.BlockSpec(memory_space=pl.ANY)] * len(sources),
        out_specs=[pl.BlockSpec(memory_space=pl.ANY)] * len(shapes),
        scratch_shapes=[pltpu.VMEM(source.shape, kind) for source in sources]
        + [pltpu.SemaphoreType.DMA((len(blocks),)), pltpu.SemaphoreType.DMA((count,))],
        compiler_params=pltpu.CompilerParams(vmem_limit_bytes=staged + (2 << 20)),
        cost_estimate=pl.CostEstimate(flops=0, bytes_accessed=2 * staged, transcendentals=0),
    )(spots, *sources)


def gather_pieces(shard):
    return [shard] + [x_shift(shard, step) for step in range(1, X)]


def both_cores(pieces, shapes, targets, each):
    xi, ci = lax.axis_index("x"), lax.axis_index("core")
    own = jnp.stack(pieces)
    spots = [((xi - k) % X) * CORES + (ci if mine else 1 - ci) for mine in (1, 0) for k in range(X)]
    return place(
        jnp.stack(spots).astype(jnp.int32),
        [own, core_swap(own)],
        shapes,
        lambda spots: [targets(spot) for spot in spots],
        CORES * X * each,
    )


def gather_dense(up_shard, down_shard):
    xi, ci, zi, yi = (lax.axis_index(name) for name in ("x", "core", "z", "y"))
    depth, width = up_shard.shape[0], down_shard.shape[1]
    up_part = lax.dynamic_slice_in_dim(up_shard, zi * width, width, axis=1)
    down_part = lax.dynamic_slice_in_dim(down_shard, yi * depth, depth, axis=0)
    pieces = gather_pieces(jnp.concatenate([up_part, down_part], axis=0))
    up_x = jnp.stack([piece[:depth] for piece in pieces])
    down_x = jnp.stack([piece[depth:] for piece in pieces])
    up_own = lax.all_gather(up_x, "z", axis=0, tiled=True)
    down_own = lax.all_gather(down_x, "y", axis=0, tiled=True)
    rows = [
        ((xi - k) % X) * CORES + (ci if mine else 1 - ci)
        for mine in (1, 0)
        for _ in range(X)
        for k in range(X)
    ]
    every = slice(None)
    count = CORES * X * X
    parts = [n // X % X for n in range(count)]

    def columns(spots):
        return [
            [((every, every), 0, (spots[n], every, pl.ds(parts[n] * width, width)))]
            for n in range(count)
        ]

    def stripes(spots):
        return [[((every, every), 0, (spots[n], parts[n]))] for n in range(count)]

    rows = jnp.stack(rows).astype(jnp.int32)
    (up,) = place(
        rows, [up_own, core_swap(up_own)], [(X * CORES, depth, X * width)], columns, count
    )
    (down,) = place(
        rows, [down_own, core_swap(down_own)], [(X * CORES, X, depth, width)], stripes, count
    )
    return up.reshape(-1, X * width), down.reshape(-1, width)


def split_rows(left):
    xi, ci = lax.axis_index("x"), lax.axis_index("core")
    rows, wide = left.shape
    blocks = left.T.reshape(X, CORES, wide // (X * CORES), rows)
    blocks = lax.dynamic_slice_in_dim(jnp.concatenate([blocks, blocks], axis=0), xi, X, axis=0)
    own = lax.dynamic_index_in_dim(blocks, ci, 1, keepdims=False)
    other = lax.dynamic_index_in_dim(blocks, 1 - ci, 1, keepdims=False)
    return own.reshape(wide // CORES, rows), other.reshape(wide // CORES, rows)


def scatter_halves(own, other):
    block = own[0].shape[0] // X
    starts = [sum(part.shape[1] for part in own[:k]) for k in range(len(own))]
    got = core_swap(jnp.concatenate([part.astype(jnp.bfloat16) for part in other], axis=1))
    totals = [
        part + got[:, start : start + part.shape[1]].astype(jnp.float32)
        for part, start in zip(own, starts)
    ]
    low = jnp.concatenate([t[block:].astype(jnp.bfloat16) for t in totals], axis=1)
    arrived = [x_shift(low[(k - 1) * block : k * block], k) for k in range(1, X)]
    sums = []
    for t, start in zip(totals, starts):
        cut = slice(start, start + t.shape[1])
        sums.append(t[:block] + sum(a[:, cut].astype(jnp.float32) for a in arrived))
    return sums


def scatter_whole(part, earlier):
    low = after(part.astype(jnp.bfloat16), earlier)
    return lax.psum_scatter(low, ("x", "core"), scatter_dimension=0, tiled=True)


def sum_over_zy(shares, small):
    spots, wide = 16, 768
    parts = []
    for share in shares:
        low = share.astype(jnp.bfloat16)
        stripes = [low[:, k : k + wide] for k in range(0, low.shape[1], wide)]
        parts.append(jnp.concatenate(stripes, axis=0).reshape(spots, -1, wide))
    if small is not None:
        last = small.astype(jnp.bfloat16).reshape(spots, -1, wide)
        parts.append(jnp.pad(last, ((0, 0), (0, 8 - last.shape[1]), (0, 0))))
    packed = jnp.concatenate(parts, axis=1)
    came = lax.all_to_all(packed, ("z", "y"), split_axis=0, concat_axis=0, tiled=True)
    mine = jnp.sum(came.astype(jnp.float32), axis=0).astype(jnp.bfloat16)
    copies = jnp.broadcast_to(mine[None], packed.shape)
    back = lax.all_to_all(copies, ("z", "y"), split_axis=0, concat_axis=0, tiled=True)
    sums, start = [], 0
    for share, part in zip(shares, parts):
        depth, high = share.shape[0], part.shape[1]
        rows = back[:, start : start + high].reshape(-1, wide).astype(jnp.float32)
        start += high
        sums.append(
            jnp.concatenate([rows[k : k + depth] for k in range(0, rows.shape[0], depth)], axis=1)
        )
    if small is None:
        return sums
    rest = back[:, start : start + last.shape[1]]
    return sums, rest.reshape(small.shape).astype(jnp.float32)


def weight_grad(left, right):
    own, other = split_rows(left)
    return product(own, right), product(other, right)


def attend_forward(stream, gain, in_proj, out_proj, images, length):
    rows, width = stream.shape
    scale = HEAD_DIM ** (-0.5)
    normed_f, saved = norm_rows(stream, gain)
    normed = normed_f.astype(jnp.bfloat16)
    joined = product(normed, in_proj).astype(jnp.bfloat16)
    query, key, value = split_heads(joined, images, length)
    scores = jnp.einsum("sqhd,skhd->shqk", query, key, preferred_element_type=jnp.float32) * scale
    top = jnp.max(scores, axis=-1, keepdims=True)
    expo = jnp.exp(scores - top)
    total = jnp.sum(expo, axis=-1, keepdims=True)
    weights = expo / total
    log_total = top + jnp.log(total)
    mixed = jnp.einsum(
        "shqk,skhd->sqhd", weights.astype(jnp.bfloat16), value, preferred_element_type=jnp.float32
    )
    mixed = mixed.reshape(rows, width).astype(jnp.bfloat16)
    return (stream + product(mixed, out_proj), (normed, saved, joined, log_total, mixed))


def attend_backward(grad, gain, in_proj, out_proj, kept, images, length, weight_grad):
    normed, saved, joined, log_total, mixed = kept
    rows, width = grad.shape
    scale = HEAD_DIM ** (-0.5)
    grad_low = grad.astype(jnp.bfloat16)
    out_grad_w = weight_grad(mixed, grad_low)
    query, key, value = split_heads(joined, images, length)
    mixed_grad = product_bt(grad_low, out_proj).astype(jnp.bfloat16).reshape(query.shape)
    scores = jnp.einsum("sqhd,skhd->shqk", query, key, preferred_element_type=jnp.float32) * scale
    weights = jnp.exp(scores - log_total)
    weight_grad_ = jnp.einsum(
        "sqhd,skhd->shqk", mixed_grad, value, preferred_element_type=jnp.float32
    )
    value_grad = jnp.einsum(
        "shqk,sqhd->skhd",
        weights.astype(jnp.bfloat16),
        mixed_grad,
        preferred_element_type=jnp.float32,
    )
    score_grad = weights * (weight_grad_ - jnp.sum(weights * weight_grad_, axis=-1, keepdims=True))
    score_grad = score_grad.astype(jnp.bfloat16)
    query_grad = (
        jnp.einsum("shqk,skhd->sqhd", score_grad, key, preferred_element_type=jnp.float32) * scale
    )
    key_grad = (
        jnp.einsum("shqk,sqhd->skhd", score_grad, query, preferred_element_type=jnp.float32) * scale
    )
    joined_grad = (
        jnp.stack([query_grad, key_grad, value_grad], axis=2)
        .reshape(rows, 3 * width)
        .astype(jnp.bfloat16)
    )
    in_grad_w = weight_grad(normed, joined_grad)
    stream_grad, gain_grad = norm_back(product_bt(joined_grad, in_proj), gain, saved)
    return (grad + stream_grad, (gain_grad, in_grad_w, out_grad_w))


def dense_forward(stream, gain, up_w, down_w):
    normed_f, saved = norm_rows(stream, gain)
    normed = normed_f.astype(jnp.bfloat16)
    hidden, slope = gelu_parts(product(normed, up_w))
    hidden = hidden.astype(jnp.bfloat16)
    return (stream + product(hidden, down_w), (normed, saved, slope, hidden))


def dense_backward(grad, gain, up_w, down_w, kept, earlier):
    normed, saved, slope, hidden = kept
    grad_low = grad.astype(jnp.bfloat16)
    pre_grad = (product_bt(grad_low, down_w) * slope).astype(jnp.bfloat16)
    up_grad = scatter_whole(product_t(normed, pre_grad), earlier)
    down_grad = scatter_whole(product_t(hidden, grad_low), earlier)
    stream_grad, gain_grad = norm_back(product_bt(pre_grad, up_w), gain, saved)
    return (grad + stream_grad, (gain_grad, up_grad, down_grad))


def moe(stream, grad_low, gain, router, up_half, down_half, routes, slot_index, keep_mask):
    rows, width = stream.shape
    experts = router.shape[1]
    slots = experts * SLOTS
    grad = grad_low.astype(jnp.float32)
    normed_f, saved = norm_rows(stream, gain)
    normed = normed_f.astype(jnp.bfloat16)
    logits = product(normed, router)
    top = jnp.max(logits, axis=-1, keepdims=True)
    expo = jnp.exp(logits - top)
    probs = expo / jnp.sum(expo, axis=-1, keepdims=True)
    expert_ids = lax.broadcasted_iota(jnp.int32, (rows, experts), 1)
    keep_float = keep_mask.astype(jnp.float32)
    keep_first, keep_second = keep_float[:, 0:1], keep_float[:, 1:2]
    hot_first = (expert_ids == routes[:, 0:1]).astype(jnp.float32)
    hot_second = (expert_ids == routes[:, 1:2]).astype(jnp.float32)
    gate_first = jnp.sum(probs * hot_first, axis=-1, keepdims=True) * keep_first
    gate_second = jnp.sum(probs * hot_second, axis=-1, keepdims=True) * keep_second
    columns = lax.broadcasted_iota(jnp.int32, (rows, slots), 1)
    target = routes * SLOTS + slot_index
    pick_first = (columns == target[:, 0:1]).astype(jnp.float32) * keep_first
    pick_second = (columns == target[:, 1:2]).astype(jnp.float32) * keep_second
    select = (pick_first + pick_second).astype(jnp.bfloat16)
    slot_gate = jnp.sum(pick_first * gate_first + pick_second * gate_second, axis=0)
    send_rows = product_t(select, normed).astype(jnp.bfloat16)
    send_grad = (product_t(select, grad_low) * slot_gate[:, None]).astype(jnp.bfloat16)
    send = jnp.concatenate(
        [send_rows.reshape(experts, SLOTS, width), send_grad.reshape(experts, SLOTS, width)], axis=1
    )
    received = lax.all_to_all(send, ("z", "y"), split_axis=0, concat_axis=0, tiled=True)
    partner = core_swap(received)

    flat = jnp.concatenate([received[:, :SLOTS], partner[:, :SLOTS]], axis=0).reshape(-1, width)
    flat_grad = jnp.concatenate([received[:, SLOTS:], partner[:, SLOTS:]], axis=0).reshape(-1, width)
    hidden, slope = gelu_parts(product_bt(flat, up_half))
    hidden = hidden.astype(jnp.bfloat16)
    partial_out = product(hidden, down_half)
    got_out = core_swap(partial_out[slots:].astype(jnp.bfloat16))
    pre_grad = (product_bt(flat_grad, down_half) * slope).astype(jnp.bfloat16)
    partial_in = product(pre_grad, up_half)
    got_in = core_swap(partial_in[slots:].astype(jnp.bfloat16))
    result = (partial_out[:slots] + got_out.astype(jnp.float32)).astype(jnp.bfloat16)
    in_grad = (partial_in[:slots] + got_in.astype(jnp.float32)).astype(jnp.bfloat16)
    back = jnp.concatenate(
        [result.reshape(experts, SLOTS, width), in_grad.reshape(experts, SLOTS, width)], axis=1
    )
    returned = lax.all_to_all(back, ("z", "y"), split_axis=0, concat_axis=0, tiled=True)
    result_rows = returned[:, :SLOTS].reshape(slots, width)
    back_rows = returned[:, SLOTS:].reshape(slots, width)

    down_low = product_t(hidden, flat_grad).astype(jnp.bfloat16)
    up_low = product_t(pre_grad, flat).astype(jnp.bfloat16)
    made = mark(down_low, up_low)
    down_grad = lax.psum_scatter(down_low, "x", scatter_dimension=0, tiled=True)
    up_grad = lax.psum_scatter(up_low, "x", scatter_dimension=0, tiled=True)
    down_grad = down_grad.astype(jnp.float32)
    up_grad = up_grad.astype(jnp.float32).T

    first = product(pick_first.astype(jnp.bfloat16), result_rows)
    second = product(pick_second.astype(jnp.bfloat16), result_rows)
    new_stream = stream + gate_first * first + gate_second * second
    gate_grad_first = jnp.sum(grad * first, axis=-1, keepdims=True) * keep_first
    gate_grad_second = jnp.sum(grad * second, axis=-1, keepdims=True) * keep_second
    probs_grad = gate_grad_first * hot_first + gate_grad_second * hot_second
    logit_grad = probs * (probs_grad - jnp.sum(probs * probs_grad, axis=-1, keepdims=True))
    logit_grad = logit_grad.astype(jnp.bfloat16)
    router_grad = product_t(normed, logit_grad)
    normed_grad = product_bt(logit_grad, router) + product(select, back_rows)
    stream_grad, gain_grad = norm_back(normed_grad, gain, saved)
    return (new_stream, grad + stream_grad, (gain_grad, router_grad, up_grad, down_grad), made)


def shards(
    tokens,
    norm_attn_a,
    in_proj_a,
    out_proj_a,
    norm_dense,
    dense_up,
    dense_down,
    norm_attn_b,
    in_proj_b,
    out_proj_b,
    norm_moe,
    router,
    expert_up,
    expert_down,
    routes,
    slot_index,
    keep_mask,
    output_grad,
):
    images, length, width = tokens.shape
    rows = images * length
    stream = tokens.reshape(rows, width).astype(jnp.float32)
    flat_routes = routes.reshape(rows, 2)
    flat_slots = slot_index.reshape(rows, 2)
    flat_keep = keep_mask.reshape(rows, 2)
    experts = router.shape[1]
    small = jnp.concatenate(
        [
            jnp.stack([norm_attn_a, norm_dense, norm_attn_b, norm_moe], axis=1),
            router,
            jnp.zeros((router.shape[0], 128 - 4 - experts), router.dtype),
        ],
        axis=1,
    )
    wide_in, wide_out = in_proj_a.shape[1], out_proj_a.shape[1]
    blocks, depth = X * CORES, in_proj_a.shape[0]
    every = slice(None)

    def side_by_side(widths):
        starts = [sum(widths[:at]) for at in range(len(widths))]
        return lambda spot: [
            ((every, pl.ds(start, wide)), at, (spot,))
            for at, (start, wide) in enumerate(zip(starts, widths))
        ]

    pieces = gather_pieces(jnp.concatenate([in_proj_a, out_proj_a, small], axis=1))
    widths = [wide_in, wide_out, 128]
    in_aa, out_aa, small_all = both_cores(
        pieces, [(blocks, depth, wide) for wide in widths], side_by_side(widths), len(widths)
    )
    in_aa, out_aa, small_all = (w.reshape(width, -1) for w in (in_aa, out_aa, small_all))
    gain_aa, gain_dd, gain_bb, gain_mm = (small_all[:, k] for k in range(4))
    router_full = small_all[:, 4 : 4 + experts]

    up_dd, down_dd = gather_dense(dense_up, dense_down)

    pieces = gather_pieces(jnp.concatenate([in_proj_b, out_proj_b], axis=1))
    widths = [wide_in, wide_out]
    in_bb, out_bb = both_cores(
        pieces, [(blocks, depth, wide) for wide in widths], side_by_side(widths), len(widths)
    )
    in_bb, out_bb = in_bb.reshape(width, -1), out_bb.reshape(width, -1)

    up_half = lax.all_gather(expert_up[0].T, "x", axis=0, tiled=True)
    down_half = lax.all_gather(expert_down[0], "x", axis=0, tiled=True)

    stream_one, kept_one = attend_forward(stream, gain_aa, in_aa, out_aa, images, length)
    stream_two, kept_two = dense_forward(stream_one, gain_dd, up_dd, down_dd)
    stream_three, kept_three = attend_forward(stream_two, gain_bb, in_bb, out_bb, images, length)
    stream_four, grad, moe_grads, made = moe(
        stream_three,
        output_grad.reshape(rows, width),
        gain_mm,
        router_full,
        up_half,
        down_half,
        flat_routes,
        flat_slots,
        flat_keep,
    )
    output = stream_four.astype(jnp.bfloat16).reshape(images, length, width)
    grad = after(grad, made)
    grad, attn_b_grads = attend_backward(
        grad, gain_bb, in_bb, out_bb, kept_three, images, length, product_t
    )
    sent = mark(moe_grads[2], moe_grads[3])
    share_b = scatter_whole(jnp.concatenate(attn_b_grads[1:], axis=1), sent)
    grad, dense_grads = dense_backward(grad, gain_dd, up_dd, down_dd, kept_two, sent)
    grad, attn_a_grads = attend_backward(
        grad, gain_aa, in_aa, out_aa, kept_one, images, length, weight_grad
    )
    input_grad = grad.reshape(images, length, width)
    small_grad = jnp.concatenate(
        [
            jnp.stack([attn_a_grads[0], dense_grads[0], attn_b_grads[0], moe_grads[0]], axis=0),
            moe_grads[1].T,
            jnp.zeros((128 - 4 - experts, width), jnp.float32),
        ],
        axis=0,
    )
    in_a, out_a, small_share = scatter_halves(
        *zip(attn_a_grads[1], attn_a_grads[2], split_rows(small_grad))
    )
    share_a = jnp.concatenate([in_a, out_a], axis=1)
    (share_a, share_b), small_total = sum_over_zy([share_a, share_b], small_share)
    up, down = sum_over_zy(dense_grads[1:], None)
    in_a, out_a = share_a[:, :wide_in], share_a[:, wide_in:]
    in_b, out_b = share_b[:, :wide_in], share_b[:, wide_in:]
    return (
        output,
        input_grad,
        small_total[:, 0],
        in_a,
        out_a,
        small_total[:, 1],
        up,
        down,
        small_total[:, 2],
        in_b,
        out_b,
        small_total[:, 3],
        small_total[:, 4 : 4 + experts],
        moe_grads[2][None],
        moe_grads[3][None],
    )


def solution(mesh):
    places = Mesh(mesh.devices.reshape(X, CORES, 4, 4), ("x", "core", "z", "y"))
    dp, expert = ("x", "core"), ("z", "y")
    images = P(dp + expert, None, None)
    return jax.shard_map(
        shards,
        mesh=places,
        in_specs=(
            images,
            P(dp),
            P(dp, None),
            P(dp, None),
            P(dp),
            P(dp, None),
            P(dp, None),
            P(dp),
            P(dp, None),
            P(dp, None),
            P(dp),
            P(dp, None),
            P(expert, None, dp),
            P(expert, dp, None),
            images,
            images,
            images,
            images,
        ),
        out_specs=(
            images,
            images,
            P(dp),
            P(dp, None),
            P(dp, None),
            P(dp),
            P(dp, None),
            P(dp, None),
            P(dp),
            P(dp, None),
            P(dp, None),
            P(dp),
            P(dp, None),
            P(expert, None, dp),
            P(expert, dp, None),
        ),
        check_vma=False,
    )
```

```python
import math

import jax
import jax.numpy as jnp
from jax import lax
from jax.experimental import pallas as pl
from jax.experimental.pallas import tpu as pltpu
from jax.sharding import Mesh, PartitionSpec as P

HEAD_DIM = 64


epsilon = 1e-06


def product(left, right):
    return jnp.dot(left, right, preferred_element_type=jnp.float32)


def product_t(left, right):
    return lax.dot_general(
        left, right, (((0,), (0,)), ((), ())), preferred_element_type=jnp.float32
    )


def product_bt(left, right):
    return lax.dot_general(
        left, right, (((1,), (1,)), ((), ())), preferred_element_type=jnp.float32
    )


def norm_rows(stream, gain):
    center = jnp.mean(stream, axis=-1, keepdims=True)
    centred = stream - center
    spread = jnp.mean(centred * centred, axis=-1, keepdims=True)
    inverse = lax.rsqrt(spread + epsilon)
    scaled = centred * inverse
    return (scaled * gain.astype(jnp.float32), (scaled, inverse))


def norm_back(grad, gain, saved):
    scaled, inverse = saved
    shifted = grad * gain.astype(jnp.float32)
    gain_grad = jnp.sum(grad * scaled, axis=0)
    inner = (
        shifted
        - jnp.mean(shifted, axis=-1, keepdims=True)
        - scaled * jnp.mean(shifted * scaled, axis=-1, keepdims=True)
    )
    return (inner * inverse, gain_grad)


def gelu_parts(value):
    normal_cdf = 0.5 * (1.0 + lax.erf(value * (1.0 / math.sqrt(2.0))))
    slope = normal_cdf + value * jnp.exp(-0.5 * value * value) * (1.0 / math.sqrt(2.0 * math.pi))
    return value * normal_cdf, slope


def split_heads(joined, images, length):
    heads = joined.shape[1] // (3 * HEAD_DIM)
    parts = joined.reshape(images, length, 3, heads, HEAD_DIM)
    return (parts[:, :, 0], parts[:, :, 1], parts[:, :, 2])


X, CORES = 4, 2
SLOTS = 32


def shift(block, axis, step):
    return lax.ppermute(block, axis, [(i, (i + step) % X) for i in range(X)])


def x_shift(block, step):
    return shift(block, "x", step)


def rolled(array, start, axis):
    doubled = jnp.concatenate([array, array], axis=axis)
    return lax.dynamic_slice_in_dim(doubled, start, X, axis=axis)


def core_swap(block):
    return lax.ppermute(block, "core", [(0, 1), (1, 0)])


def after(block, earlier):
    return jnp.where(earlier == earlier, block, jnp.zeros_like(block))


def mark(*blocks):
    return sum(block[(0,) * block.ndim].astype(jnp.float32) for block in blocks)


def place(spots, sources, shapes, moves, count):
    kind = sources[0].dtype
    blocks = [(n, k) for n, source in enumerate(sources) for k in range(source.shape[0])]
    staged = 2 * sum(math.prod(source.shape) for source in sources)

    def kernel(spots_ref, *refs):
        ins, refs = refs[: len(sources)], refs[len(sources) :]
        outs, refs = refs[: len(shapes)], refs[len(shapes) :]
        stages, (in_sems, out_sems) = refs[: len(sources)], refs[len(sources) :]
        loads = [
            pltpu.make_async_copy(ins[n].at[k], stages[n].at[k], in_sems.at[at])
            for at, (n, k) in enumerate(blocks)
        ]
        for load in loads:
            load.start()
        stores = []
        listed = moves([spots_ref[k] for k in range(spots.shape[0])])
        for load, (n, k), targets in zip(loads, blocks, listed):
            load.wait()
            for cut, at, spot in targets:
                store = pltpu.make_async_copy(
                    stages[n].at[(k,) + cut], outs[at].at[spot], out_sems.at[len(stores)]
                )
                store.start()
                stores.append(store)
        for store in stores:
            store.wait()

    return pl.pallas_call(
        kernel,
        out_shape=[jax.ShapeDtypeStruct(shape, kind) for shape in shapes],
        in_specs=[pl.BlockSpec(memory_space=pltpu.SMEM)]
        + [pl.BlockSpec(memory_space=pl.ANY)] * len(sources),
        out_specs=[pl.BlockSpec(memory_space=pl.ANY)] * len(shapes),
        scratch_shapes=[pltpu.VMEM(source.shape, kind) for source in sources]
        + [pltpu.SemaphoreType.DMA((len(blocks),)), pltpu.SemaphoreType.DMA((count,))],
        compiler_params=pltpu.CompilerParams(vmem_limit_bytes=staged + (2 << 20)),
        cost_estimate=pl.CostEstimate(flops=0, bytes_accessed=2 * staged, transcendentals=0),
    )(spots, *sources)


def gather_pieces(shard):
    return [shard] + [x_shift(shard, step) for step in range(1, X)]


def both_cores(pieces, shapes, targets, each):
    xi, ci = lax.axis_index("x"), lax.axis_index("core")
    own = jnp.stack(pieces)
    spots = [((xi - k) % X) * CORES + (ci if mine else 1 - ci) for mine in (1, 0) for k in range(X)]
    return place(
        jnp.stack(spots).astype(jnp.int32),
        [own, core_swap(own)],
        shapes,
        lambda spots: [targets(spot) for spot in spots],
        CORES * X * each,
    )


def gather_dense(up_shard, down_shard):
    xi, ci, zi, yi = (lax.axis_index(name) for name in ("x", "core", "z", "y"))
    depth, width = up_shard.shape[0], down_shard.shape[1]
    up_part = lax.dynamic_slice_in_dim(up_shard, zi * width, width, axis=1)
    down_part = lax.dynamic_slice_in_dim(down_shard, yi * depth, depth, axis=0)
    pieces = gather_pieces(jnp.concatenate([up_part, down_part], axis=0))
    up_x = jnp.stack([piece[:depth] for piece in pieces])
    down_x = jnp.stack([piece[depth:] for piece in pieces])
    up_own = lax.all_gather(up_x, "z", axis=0, tiled=True)
    down_own = lax.all_gather(down_x, "y", axis=0, tiled=True)
    rows = [
        ((xi - k) % X) * CORES + (ci if mine else 1 - ci)
        for mine in (1, 0)
        for _ in range(X)
        for k in range(X)
    ]
    every = slice(None)
    count = CORES * X * X
    parts = [n // X % X for n in range(count)]

    def columns(spots):
        return [
            [((every, every), 0, (spots[n], every, pl.ds(parts[n] * width, width)))]
            for n in range(count)
        ]

    def stripes(spots):
        return [[((every, every), 0, (spots[n], parts[n]))] for n in range(count)]

    rows = jnp.stack(rows).astype(jnp.int32)
    (up,) = place(
        rows, [up_own, core_swap(up_own)], [(X * CORES, depth, X * width)], columns, count
    )
    (down,) = place(
        rows, [down_own, core_swap(down_own)], [(X * CORES, X, depth, width)], stripes, count
    )
    return up.reshape(-1, X * width), down.reshape(-1, width)


def split_rows(left):
    xi, ci = lax.axis_index("x"), lax.axis_index("core")
    rows, wide = left.shape
    blocks = left.T.reshape(X, CORES, wide // (X * CORES), rows)
    blocks = lax.dynamic_slice_in_dim(jnp.concatenate([blocks, blocks], axis=0), xi, X, axis=0)
    own = lax.dynamic_index_in_dim(blocks, ci, 1, keepdims=False)
    other = lax.dynamic_index_in_dim(blocks, 1 - ci, 1, keepdims=False)
    return own.reshape(wide // CORES, rows), other.reshape(wide // CORES, rows)


def scatter_halves(own, other):
    block = own[0].shape[0] // X
    starts = [sum(part.shape[1] for part in own[:k]) for k in range(len(own))]
    got = core_swap(jnp.concatenate([part.astype(jnp.bfloat16) for part in other], axis=1))
    totals = [
        part + got[:, start : start + part.shape[1]].astype(jnp.float32)
        for part, start in zip(own, starts)
    ]
    low = jnp.concatenate([t[block:].astype(jnp.bfloat16) for t in totals], axis=1)
    arrived = [x_shift(low[(k - 1) * block : k * block], k) for k in range(1, X)]
    sums = []
    for t, start in zip(totals, starts):
        cut = slice(start, start + t.shape[1])
        sums.append(t[:block] + sum(a[:, cut].astype(jnp.float32) for a in arrived))
    return sums


def scatter_whole(part):
    return lax.psum_scatter(
        part.astype(jnp.bfloat16), ("x", "core"), scatter_dimension=0, tiled=True
    )


def sum_over_zy(shares, small):
    spots, wide = 16, 768
    parts = []
    for share in shares:
        low = share.astype(jnp.bfloat16)
        stripes = [low[:, k : k + wide] for k in range(0, low.shape[1], wide)]
        parts.append(jnp.concatenate(stripes, axis=0).reshape(spots, -1, wide))
    if small is not None:
        last = small.astype(jnp.bfloat16).reshape(spots, -1, wide)
        parts.append(jnp.pad(last, ((0, 0), (0, 8 - last.shape[1]), (0, 0))))
    packed = jnp.concatenate(parts, axis=1)
    came = lax.all_to_all(packed, ("z", "y"), split_axis=0, concat_axis=0, tiled=True)
    mine = jnp.sum(came.astype(jnp.float32), axis=0).astype(jnp.bfloat16)
    copies = jnp.broadcast_to(mine[None], packed.shape)
    back = lax.all_to_all(copies, ("z", "y"), split_axis=0, concat_axis=0, tiled=True)
    sums, start = [], 0
    for share, part in zip(shares, parts):
        depth, high = share.shape[0], part.shape[1]
        rows = back[:, start : start + high].reshape(-1, wide).astype(jnp.float32)
        start += high
        sums.append(
            jnp.concatenate([rows[k : k + depth] for k in range(0, rows.shape[0], depth)], axis=1)
        )
    if small is None:
        return sums
    rest = back[:, start : start + last.shape[1]]
    return sums, rest.reshape(small.shape).astype(jnp.float32)


def weight_grad(left, right):
    own, other = split_rows(left)
    return product(own, right), product(other, right)


def attend_forward(stream, gain, in_proj, out_proj, images, length):
    rows, width = stream.shape
    scale = HEAD_DIM ** (-0.5)
    normed_f, saved = norm_rows(stream, gain)
    normed = normed_f.astype(jnp.bfloat16)
    joined = product(normed, in_proj).astype(jnp.bfloat16)
    query, key, value = split_heads(joined, images, length)
    scores = jnp.einsum("sqhd,skhd->shqk", query, key, preferred_element_type=jnp.float32) * scale
    top = jnp.max(scores, axis=-1, keepdims=True)
    expo = jnp.exp(scores - top)
    total = jnp.sum(expo, axis=-1, keepdims=True)
    weights = expo / total
    log_total = top + jnp.log(total)
    mixed = jnp.einsum(
        "shqk,skhd->sqhd", weights.astype(jnp.bfloat16), value, preferred_element_type=jnp.float32
    )
    mixed = mixed.reshape(rows, width).astype(jnp.bfloat16)
    return (stream + product(mixed, out_proj), (normed, saved, joined, log_total, mixed))


def attend_backward(grad, gain, in_proj, out_proj, kept, images, length, weight_grad):
    normed, saved, joined, log_total, mixed = kept
    rows, width = grad.shape
    scale = HEAD_DIM ** (-0.5)
    grad_low = grad.astype(jnp.bfloat16)
    out_grad_w = weight_grad(mixed, grad_low)
    query, key, value = split_heads(joined, images, length)
    mixed_grad = product_bt(grad_low, out_proj).astype(jnp.bfloat16).reshape(query.shape)
    scores = jnp.einsum("sqhd,skhd->shqk", query, key, preferred_element_type=jnp.float32) * scale
    weights = jnp.exp(scores - log_total)
    weight_grad_ = jnp.einsum(
        "sqhd,skhd->shqk", mixed_grad, value, preferred_element_type=jnp.float32
    )
    value_grad = jnp.einsum(
        "shqk,sqhd->skhd",
        weights.astype(jnp.bfloat16),
        mixed_grad,
        preferred_element_type=jnp.float32,
    )
    score_grad = weights * (weight_grad_ - jnp.sum(weights * weight_grad_, axis=-1, keepdims=True))
    score_grad = score_grad.astype(jnp.bfloat16)
    query_grad = (
        jnp.einsum("shqk,skhd->sqhd", score_grad, key, preferred_element_type=jnp.float32) * scale
    )
    key_grad = (
        jnp.einsum("shqk,sqhd->skhd", score_grad, query, preferred_element_type=jnp.float32) * scale
    )
    joined_grad = (
        jnp.stack([query_grad, key_grad, value_grad], axis=2)
        .reshape(rows, 3 * width)
        .astype(jnp.bfloat16)
    )
    in_grad_w = weight_grad(normed, joined_grad)
    stream_grad, gain_grad = norm_back(product_bt(joined_grad, in_proj), gain, saved)
    return (grad + stream_grad, (gain_grad, in_grad_w, out_grad_w))


def dense_forward(stream, gain, up_w, down_w):
    normed_f, saved = norm_rows(stream, gain)
    normed = normed_f.astype(jnp.bfloat16)
    hidden, slope = gelu_parts(product(normed, up_w))
    hidden = hidden.astype(jnp.bfloat16)
    return (stream + product(hidden, down_w), (normed, saved, slope, hidden))


def dense_backward(grad, gain, up_w, down_w, kept, earlier):
    normed, saved, slope, hidden = kept
    grad_low = grad.astype(jnp.bfloat16)
    pre_grad = (product_bt(grad_low, down_w) * slope).astype(jnp.bfloat16)
    up_grad = scatter_whole(product_t(after(normed, earlier), pre_grad))
    down_grad = scatter_whole(product_t(hidden, after(grad_low, earlier)))
    stream_grad, gain_grad = norm_back(product_bt(pre_grad, up_w), gain, saved)
    return (grad + stream_grad, (gain_grad, up_grad, down_grad))


def moe(stream, grad_low, gain, router, up_half, down_half, routes, slot_index, keep_mask):
    rows, width = stream.shape
    experts = router.shape[1]
    slots = experts * SLOTS
    grad = grad_low.astype(jnp.float32)
    normed_f, saved = norm_rows(stream, gain)
    normed = normed_f.astype(jnp.bfloat16)
    logits = product(normed, router)
    top = jnp.max(logits, axis=-1, keepdims=True)
    expo = jnp.exp(logits - top)
    probs = expo / jnp.sum(expo, axis=-1, keepdims=True)
    expert_ids = lax.broadcasted_iota(jnp.int32, (rows, experts), 1)
    keep_float = keep_mask.astype(jnp.float32)
    keep_first, keep_second = keep_float[:, 0:1], keep_float[:, 1:2]
    hot_first = (expert_ids == routes[:, 0:1]).astype(jnp.float32)
    hot_second = (expert_ids == routes[:, 1:2]).astype(jnp.float32)
    gate_first = jnp.sum(probs * hot_first, axis=-1, keepdims=True) * keep_first
    gate_second = jnp.sum(probs * hot_second, axis=-1, keepdims=True) * keep_second
    columns = lax.broadcasted_iota(jnp.int32, (rows, slots), 1)
    target = routes * SLOTS + slot_index
    pick_first = (columns == target[:, 0:1]).astype(jnp.float32) * keep_first
    pick_second = (columns == target[:, 1:2]).astype(jnp.float32) * keep_second
    select = (pick_first + pick_second).astype(jnp.bfloat16)
    slot_gate = jnp.sum(pick_first * gate_first + pick_second * gate_second, axis=0)
    send_rows = product_t(select, normed).astype(jnp.bfloat16)
    send_grad = (product_t(select, grad_low) * slot_gate[:, None]).astype(jnp.bfloat16)
    send = jnp.concatenate(
        [send_rows.reshape(experts, SLOTS, width), send_grad.reshape(experts, SLOTS, width)], axis=1
    )
    received = lax.all_to_all(send, ("z", "y"), split_axis=0, concat_axis=0, tiled=True)
    partner = core_swap(received)

    flat = jnp.concatenate([received[:, :SLOTS], partner[:, :SLOTS]], axis=0).reshape(-1, width)
    flat_grad = jnp.concatenate([received[:, SLOTS:], partner[:, SLOTS:]], axis=0).reshape(-1, width)
    hidden, slope = gelu_parts(product_bt(flat, up_half))
    hidden = hidden.astype(jnp.bfloat16)
    partial_out = product(hidden, down_half)
    got_out = core_swap(partial_out[slots:].astype(jnp.bfloat16))
    pre_grad = (product_bt(flat_grad, down_half) * slope).astype(jnp.bfloat16)
    partial_in = product(pre_grad, up_half)
    got_in = core_swap(partial_in[slots:].astype(jnp.bfloat16))
    result = (partial_out[:slots] + got_out.astype(jnp.float32)).astype(jnp.bfloat16)
    in_grad = (partial_in[:slots] + got_in.astype(jnp.float32)).astype(jnp.bfloat16)
    back = jnp.concatenate(
        [result.reshape(experts, SLOTS, width), in_grad.reshape(experts, SLOTS, width)], axis=1
    )
    returned = lax.all_to_all(back, ("z", "y"), split_axis=0, concat_axis=0, tiled=True)
    result_rows = returned[:, :SLOTS].reshape(slots, width)
    back_rows = returned[:, SLOTS:].reshape(slots, width)

    down_low = product_t(hidden, flat_grad).astype(jnp.bfloat16)
    up_low = product_t(pre_grad, flat).astype(jnp.bfloat16)
    made = mark(down_low, up_low)
    down_grad = lax.psum_scatter(down_low, "x", scatter_dimension=0, tiled=True)
    up_grad = lax.psum_scatter(up_low, "x", scatter_dimension=0, tiled=True)
    down_grad = down_grad.astype(jnp.float32)
    up_grad = up_grad.astype(jnp.float32).T

    first = product(pick_first.astype(jnp.bfloat16), result_rows)
    second = product(pick_second.astype(jnp.bfloat16), result_rows)
    new_stream = stream + gate_first * first + gate_second * second
    gate_grad_first = jnp.sum(grad * first, axis=-1, keepdims=True) * keep_first
    gate_grad_second = jnp.sum(grad * second, axis=-1, keepdims=True) * keep_second
    probs_grad = gate_grad_first * hot_first + gate_grad_second * hot_second
    logit_grad = probs * (probs_grad - jnp.sum(probs * probs_grad, axis=-1, keepdims=True))
    logit_grad = logit_grad.astype(jnp.bfloat16)
    router_grad = product_t(normed, logit_grad)
    normed_grad = product_bt(logit_grad, router) + product(select, back_rows)
    stream_grad, gain_grad = norm_back(normed_grad, gain, saved)
    return (new_stream, grad + stream_grad, (gain_grad, router_grad, up_grad, down_grad), made)


def shards(
    tokens,
    norm_attn_a,
    in_proj_a,
    out_proj_a,
    norm_dense,
    dense_up,
    dense_down,
    norm_attn_b,
    in_proj_b,
    out_proj_b,
    norm_moe,
    router,
    expert_up,
    expert_down,
    routes,
    slot_index,
    keep_mask,
    output_grad,
):
    images, length, width = tokens.shape
    rows = images * length
    stream = tokens.reshape(rows, width).astype(jnp.float32)
    flat_routes = routes.reshape(rows, 2)
    flat_slots = slot_index.reshape(rows, 2)
    flat_keep = keep_mask.reshape(rows, 2)
    experts = router.shape[1]
    small = jnp.concatenate(
        [
            jnp.stack([norm_attn_a, norm_dense, norm_attn_b, norm_moe], axis=1),
            router,
            jnp.zeros((router.shape[0], 128 - 4 - experts), router.dtype),
        ],
        axis=1,
    )
    wide_in, wide_out = in_proj_a.shape[1], out_proj_a.shape[1]
    blocks, depth = X * CORES, in_proj_a.shape[0]
    every = slice(None)

    def side_by_side(widths):
        starts = [sum(widths[:at]) for at in range(len(widths))]
        return lambda spot: [
            ((every, pl.ds(start, wide)), at, (spot,))
            for at, (start, wide) in enumerate(zip(starts, widths))
        ]

    pieces = gather_pieces(jnp.concatenate([in_proj_a, out_proj_a, small], axis=1))
    widths = [wide_in, wide_out, 128]
    in_aa, out_aa, small_all = both_cores(
        pieces, [(blocks, depth, wide) for wide in widths], side_by_side(widths), len(widths)
    )
    in_aa, out_aa, small_all = (w.reshape(width, -1) for w in (in_aa, out_aa, small_all))
    gain_aa, gain_dd, gain_bb, gain_mm = (small_all[:, k] for k in range(4))
    router_full = small_all[:, 4 : 4 + experts]

    up_dd, down_dd = gather_dense(dense_up, dense_down)

    pieces = gather_pieces(jnp.concatenate([in_proj_b, out_proj_b], axis=1))
    widths = [wide_in, wide_out]
    in_bb, out_bb = both_cores(
        pieces, [(blocks, depth, wide) for wide in widths], side_by_side(widths), len(widths)
    )
    in_bb, out_bb = in_bb.reshape(width, -1), out_bb.reshape(width, -1)

    up_half = lax.all_gather(expert_up[0].T, "x", axis=0, tiled=True)
    down_half = lax.all_gather(expert_down[0], "x", axis=0, tiled=True)

    stream_one, kept_one = attend_forward(stream, gain_aa, in_aa, out_aa, images, length)
    stream_two, kept_two = dense_forward(stream_one, gain_dd, up_dd, down_dd)
    stream_three, kept_three = attend_forward(stream_two, gain_bb, in_bb, out_bb, images, length)
    stream_four, grad, moe_grads, made = moe(
        stream_three,
        output_grad.reshape(rows, width),
        gain_mm,
        router_full,
        up_half,
        down_half,
        flat_routes,
        flat_slots,
        flat_keep,
    )
    output = stream_four.astype(jnp.bfloat16).reshape(images, length, width)
    sent = mark(moe_grads[2], moe_grads[3])

    def late_product(left, right):
        return product_t(after(left, sent), right)

    grad = after(grad, made)
    grad, attn_b_grads = attend_backward(
        grad, gain_bb, in_bb, out_bb, kept_three, images, length, late_product
    )
    share_b = scatter_whole(jnp.concatenate(attn_b_grads[1:], axis=1))
    grad, dense_grads = dense_backward(grad, gain_dd, up_dd, down_dd, kept_two, sent)
    grad, attn_a_grads = attend_backward(
        grad, gain_aa, in_aa, out_aa, kept_one, images, length, weight_grad
    )
    input_grad = grad.reshape(images, length, width)
    small_grad = jnp.concatenate(
        [
            jnp.stack([attn_a_grads[0], dense_grads[0], attn_b_grads[0], moe_grads[0]], axis=0),
            moe_grads[1].T,
            jnp.zeros((128 - 4 - experts, width), jnp.float32),
        ],
        axis=0,
    )
    in_a, out_a, small_share = scatter_halves(
        *zip(attn_a_grads[1], attn_a_grads[2], split_rows(small_grad))
    )
    share_a = jnp.concatenate([in_a, out_a], axis=1)
    (share_a, share_b, down), small_total = sum_over_zy(
        [share_a, share_b, dense_grads[2]], small_share
    )
    (up,) = sum_over_zy([after(dense_grads[1], mark(share_a))], None)
    in_a, out_a = share_a[:, :wide_in], share_a[:, wide_in:]
    in_b, out_b = share_b[:, :wide_in], share_b[:, wide_in:]
    return (
        output,
        input_grad,
        small_total[:, 0],
        in_a,
        out_a,
        small_total[:, 1],
        up,
        down,
        small_total[:, 2],
        in_b,
        out_b,
        small_total[:, 3],
        small_total[:, 4 : 4 + experts],
        moe_grads[2][None],
        moe_grads[3][None],
    )


def solution(mesh):
    places = Mesh(mesh.devices.reshape(X, CORES, 4, 4), ("x", "core", "z", "y"))
    dp, expert = ("x", "core"), ("z", "y")
    images = P(dp + expert, None, None)
    return jax.shard_map(
        shards,
        mesh=places,
        in_specs=(
            images,
            P(dp),
            P(dp, None),
            P(dp, None),
            P(dp),
            P(dp, None),
            P(dp, None),
            P(dp),
            P(dp, None),
            P(dp, None),
            P(dp),
            P(dp, None),
            P(expert, None, dp),
            P(expert, dp, None),
            images,
            images,
            images,
            images,
        ),
        out_specs=(
            images,
            images,
            P(dp),
            P(dp, None),
            P(dp, None),
            P(dp),
            P(dp, None),
            P(dp, None),
            P(dp),
            P(dp, None),
            P(dp, None),
            P(dp),
            P(dp, None),
            P(expert, None, dp),
            P(expert, dp, None),
        ),
        check_vma=False,
    )
```

```python
import math

import jax
import jax.numpy as jnp
from jax import lax
from jax.experimental import pallas as pl
from jax.experimental.pallas import tpu as pltpu
from jax.sharding import Mesh, PartitionSpec as P

HEAD_DIM = 64


epsilon = 1e-06


def product(left, right):
    return jnp.dot(left, right, preferred_element_type=jnp.float32)


def product_t(left, right):
    return lax.dot_general(
        left, right, (((0,), (0,)), ((), ())), preferred_element_type=jnp.float32
    )


def product_bt(left, right):
    return lax.dot_general(
        left, right, (((1,), (1,)), ((), ())), preferred_element_type=jnp.float32
    )


def norm_rows(stream, gain):
    center = jnp.mean(stream, axis=-1, keepdims=True)
    centred = stream - center
    spread = jnp.mean(centred * centred, axis=-1, keepdims=True)
    inverse = lax.rsqrt(spread + epsilon)
    scaled = centred * inverse
    return (scaled * gain.astype(jnp.float32), (scaled, inverse))


def norm_back(grad, gain, saved):
    scaled, inverse = saved
    shifted = grad * gain.astype(jnp.float32)
    gain_grad = jnp.sum(grad * scaled, axis=0)
    inner = (
        shifted
        - jnp.mean(shifted, axis=-1, keepdims=True)
        - scaled * jnp.mean(shifted * scaled, axis=-1, keepdims=True)
    )
    return (inner * inverse, gain_grad)


def gelu_parts(value):
    normal_cdf = 0.5 * (1.0 + lax.erf(value * (1.0 / math.sqrt(2.0))))
    slope = normal_cdf + value * jnp.exp(-0.5 * value * value) * (1.0 / math.sqrt(2.0 * math.pi))
    return value * normal_cdf, slope


def split_heads(joined, images, length):
    heads = joined.shape[1] // (3 * HEAD_DIM)
    parts = joined.reshape(images, length, 3, heads, HEAD_DIM)
    return (parts[:, :, 0], parts[:, :, 1], parts[:, :, 2])


X, CORES = 4, 2
SLOTS = 32


def shift(block, axis, step):
    return lax.ppermute(block, axis, [(i, (i + step) % X) for i in range(X)])


def x_shift(block, step):
    return shift(block, "x", step)


def rolled(array, start, axis):
    doubled = jnp.concatenate([array, array], axis=axis)
    return lax.dynamic_slice_in_dim(doubled, start, X, axis=axis)


def core_swap(block):
    return lax.ppermute(block, "core", [(0, 1), (1, 0)])


def after(block, earlier):
    return jnp.where(earlier == earlier, block, jnp.zeros_like(block))


def mark(*blocks):
    return sum(block[(0,) * block.ndim].astype(jnp.float32) for block in blocks)


def place(spots, sources, shapes, moves, count):
    kind = sources[0].dtype
    blocks = [(n, k) for n, source in enumerate(sources) for k in range(source.shape[0])]
    staged = 2 * sum(math.prod(source.shape) for source in sources)

    def kernel(spots_ref, *refs):
        ins, refs = refs[: len(sources)], refs[len(sources) :]
        outs, refs = refs[: len(shapes)], refs[len(shapes) :]
        stages, (in_sems, out_sems) = refs[: len(sources)], refs[len(sources) :]
        loads = [
            pltpu.make_async_copy(ins[n].at[k], stages[n].at[k], in_sems.at[at])
            for at, (n, k) in enumerate(blocks)
        ]
        for load in loads:
            load.start()
        stores = []
        listed = moves([spots_ref[k] for k in range(spots.shape[0])])
        for load, (n, k), targets in zip(loads, blocks, listed):
            load.wait()
            for cut, at, spot in targets:
                store = pltpu.make_async_copy(
                    stages[n].at[(k,) + cut], outs[at].at[spot], out_sems.at[len(stores)]
                )
                store.start()
                stores.append(store)
        for store in stores:
            store.wait()

    return pl.pallas_call(
        kernel,
        out_shape=[jax.ShapeDtypeStruct(shape, kind) for shape in shapes],
        in_specs=[pl.BlockSpec(memory_space=pltpu.SMEM)]
        + [pl.BlockSpec(memory_space=pl.ANY)] * len(sources),
        out_specs=[pl.BlockSpec(memory_space=pl.ANY)] * len(shapes),
        scratch_shapes=[pltpu.VMEM(source.shape, kind) for source in sources]
        + [pltpu.SemaphoreType.DMA((len(blocks),)), pltpu.SemaphoreType.DMA((count,))],
        compiler_params=pltpu.CompilerParams(vmem_limit_bytes=staged + (2 << 20)),
        cost_estimate=pl.CostEstimate(flops=0, bytes_accessed=2 * staged, transcendentals=0),
    )(spots, *sources)


def gather_pieces(shard):
    return [shard] + [x_shift(shard, step) for step in range(1, X)]


def both_cores(pieces, shapes, targets, each):
    xi, ci = lax.axis_index("x"), lax.axis_index("core")
    own = jnp.stack(pieces)
    spots = [((xi - k) % X) * CORES + (ci if mine else 1 - ci) for mine in (1, 0) for k in range(X)]
    return place(
        jnp.stack(spots).astype(jnp.int32),
        [own, core_swap(own)],
        shapes,
        lambda spots: [targets(spot) for spot in spots],
        CORES * X * each,
    )


def gather_dense(up_shard, down_shard):
    xi, ci, zi, yi = (lax.axis_index(name) for name in ("x", "core", "z", "y"))
    depth, width = up_shard.shape[0], down_shard.shape[1]
    up_part = lax.dynamic_slice_in_dim(up_shard, zi * width, width, axis=1)
    down_part = lax.dynamic_slice_in_dim(down_shard, yi * depth, depth, axis=0)
    pieces = gather_pieces(jnp.concatenate([up_part, down_part], axis=0))
    up_x = jnp.stack([piece[:depth] for piece in pieces])
    down_x = jnp.stack([piece[depth:] for piece in pieces])
    up_own = lax.all_gather(up_x, "z", axis=0, tiled=True)
    down_own = lax.all_gather(down_x, "y", axis=0, tiled=True)
    rows = [
        ((xi - k) % X) * CORES + (ci if mine else 1 - ci)
        for mine in (1, 0)
        for _ in range(X)
        for k in range(X)
    ]
    every = slice(None)
    count = CORES * X * X
    parts = [n // X % X for n in range(count)]

    def columns(spots):
        return [
            [((every, every), 0, (spots[n], every, pl.ds(parts[n] * width, width)))]
            for n in range(count)
        ]

    def stripes(spots):
        return [[((every, every), 0, (spots[n], parts[n]))] for n in range(count)]

    rows = jnp.stack(rows).astype(jnp.int32)
    (up,) = place(
        rows, [up_own, core_swap(up_own)], [(X * CORES, depth, X * width)], columns, count
    )
    (down,) = place(
        rows, [down_own, core_swap(down_own)], [(X * CORES, X, depth, width)], stripes, count
    )
    return up.reshape(-1, X * width), down.reshape(-1, width)


def split_rows(left):
    xi, ci = lax.axis_index("x"), lax.axis_index("core")
    rows, wide = left.shape
    blocks = left.T.reshape(X, CORES, wide // (X * CORES), rows)
    blocks = lax.dynamic_slice_in_dim(jnp.concatenate([blocks, blocks], axis=0), xi, X, axis=0)
    own = lax.dynamic_index_in_dim(blocks, ci, 1, keepdims=False)
    other = lax.dynamic_index_in_dim(blocks, 1 - ci, 1, keepdims=False)
    return own.reshape(wide // CORES, rows), other.reshape(wide // CORES, rows)


def scatter_halves(own, other):
    block = own[0].shape[0] // X
    starts = [sum(part.shape[1] for part in own[:k]) for k in range(len(own))]
    got = core_swap(jnp.concatenate([part.astype(jnp.bfloat16) for part in other], axis=1))
    totals = [
        part + got[:, start : start + part.shape[1]].astype(jnp.float32)
        for part, start in zip(own, starts)
    ]
    low = jnp.concatenate([t[block:].astype(jnp.bfloat16) for t in totals], axis=1)
    arrived = [x_shift(low[(k - 1) * block : k * block], k) for k in range(1, X)]
    sums = []
    for t, start in zip(totals, starts):
        cut = slice(start, start + t.shape[1])
        sums.append(t[:block] + sum(a[:, cut].astype(jnp.float32) for a in arrived))
    return sums


def scatter_whole(part):
    return lax.psum_scatter(
        part.astype(jnp.bfloat16), ("x", "core"), scatter_dimension=0, tiled=True
    )


def sum_over_zy(shares, small):
    spots, wide = 16, 768
    parts = []
    for share in shares:
        low = share.astype(jnp.bfloat16)
        stripes = [low[:, k : k + wide] for k in range(0, low.shape[1], wide)]
        parts.append(jnp.concatenate(stripes, axis=0).reshape(spots, -1, wide))
    if small is not None:
        last = small.astype(jnp.bfloat16).reshape(spots, -1, wide)
        parts.append(jnp.pad(last, ((0, 0), (0, 8 - last.shape[1]), (0, 0))))
    packed = jnp.concatenate(parts, axis=1)
    came = lax.all_to_all(packed, ("z", "y"), split_axis=0, concat_axis=0, tiled=True)
    mine = jnp.sum(came.astype(jnp.float32), axis=0).astype(jnp.bfloat16)
    copies = jnp.broadcast_to(mine[None], packed.shape)
    back = lax.all_to_all(copies, ("z", "y"), split_axis=0, concat_axis=0, tiled=True)
    sums, start = [], 0
    for share, part in zip(shares, parts):
        depth, high = share.shape[0], part.shape[1]
        rows = back[:, start : start + high].reshape(-1, wide).astype(jnp.float32)
        start += high
        sums.append(
            jnp.concatenate([rows[k : k + depth] for k in range(0, rows.shape[0], depth)], axis=1)
        )
    if small is None:
        return sums
    rest = back[:, start : start + last.shape[1]]
    return sums, rest.reshape(small.shape).astype(jnp.float32)


def weight_grad(left, right):
    own, other = split_rows(left)
    return product(own, right), product(other, right)


def attend_forward(stream, gain, in_proj, out_proj, images, length):
    rows, width = stream.shape
    scale = HEAD_DIM ** (-0.5)
    normed_f, saved = norm_rows(stream, gain)
    normed = normed_f.astype(jnp.bfloat16)
    joined = product(normed, in_proj).astype(jnp.bfloat16)
    query, key, value = split_heads(joined, images, length)
    scores = jnp.einsum("sqhd,skhd->shqk", query, key, preferred_element_type=jnp.float32) * scale
    top = jnp.max(scores, axis=-1, keepdims=True)
    expo = jnp.exp(scores - top)
    total = jnp.sum(expo, axis=-1, keepdims=True)
    weights = expo / total
    log_total = top + jnp.log(total)
    mixed = jnp.einsum(
        "shqk,skhd->sqhd", weights.astype(jnp.bfloat16), value, preferred_element_type=jnp.float32
    )
    mixed = mixed.reshape(rows, width).astype(jnp.bfloat16)
    return (stream + product(mixed, out_proj), (normed, saved, joined, log_total, mixed))


def attend_backward(grad, gain, in_proj, out_proj, kept, images, length, weight_grad):
    normed, saved, joined, log_total, mixed = kept
    rows, width = grad.shape
    scale = HEAD_DIM ** (-0.5)
    grad_low = grad.astype(jnp.bfloat16)
    out_grad_w = weight_grad(mixed, grad_low)
    query, key, value = split_heads(joined, images, length)
    mixed_grad = product_bt(grad_low, out_proj).astype(jnp.bfloat16).reshape(query.shape)
    scores = jnp.einsum("sqhd,skhd->shqk", query, key, preferred_element_type=jnp.float32) * scale
    weights = jnp.exp(scores - log_total)
    weight_grad_ = jnp.einsum(
        "sqhd,skhd->shqk", mixed_grad, value, preferred_element_type=jnp.float32
    )
    value_grad = jnp.einsum(
        "shqk,sqhd->skhd",
        weights.astype(jnp.bfloat16),
        mixed_grad,
        preferred_element_type=jnp.float32,
    )
    score_grad = weights * (weight_grad_ - jnp.sum(weights * weight_grad_, axis=-1, keepdims=True))
    score_grad = score_grad.astype(jnp.bfloat16)
    query_grad = (
        jnp.einsum("shqk,skhd->sqhd", score_grad, key, preferred_element_type=jnp.float32) * scale
    )
    key_grad = (
        jnp.einsum("shqk,sqhd->skhd", score_grad, query, preferred_element_type=jnp.float32) * scale
    )
    joined_grad = (
        jnp.stack([query_grad, key_grad, value_grad], axis=2)
        .reshape(rows, 3 * width)
        .astype(jnp.bfloat16)
    )
    in_grad_w = weight_grad(normed, joined_grad)
    stream_grad, gain_grad = norm_back(product_bt(joined_grad, in_proj), gain, saved)
    return (grad + stream_grad, (gain_grad, in_grad_w, out_grad_w))


def dense_forward(stream, gain, up_w, down_w):
    normed_f, saved = norm_rows(stream, gain)
    normed = normed_f.astype(jnp.bfloat16)
    hidden, slope = gelu_parts(product(normed, up_w))
    hidden = hidden.astype(jnp.bfloat16)
    return (stream + product(hidden, down_w), (normed, saved, slope, hidden))


def dense_backward(grad, gain, up_w, down_w, kept, earlier):
    normed, saved, slope, hidden = kept
    grad_low = grad.astype(jnp.bfloat16)
    pre_grad = (product_bt(grad_low, down_w) * slope).astype(jnp.bfloat16)
    up_grad = scatter_whole(product_t(after(normed, earlier), pre_grad))
    down_grad = scatter_whole(product_t(hidden, after(grad_low, earlier)))
    stream_grad, gain_grad = norm_back(product_bt(pre_grad, up_w), gain, saved)
    return (grad + stream_grad, (gain_grad, up_grad, down_grad))


def moe(stream, grad_low, gain, router, up_half, down_half, routes, slot_index, keep_mask):
    rows, width = stream.shape
    experts = router.shape[1]
    slots = experts * SLOTS
    grad = grad_low.astype(jnp.float32)
    normed_f, saved = norm_rows(stream, gain)
    normed = normed_f.astype(jnp.bfloat16)
    logits = product(normed, router)
    top = jnp.max(logits, axis=-1, keepdims=True)
    expo = jnp.exp(logits - top)
    probs = expo / jnp.sum(expo, axis=-1, keepdims=True)
    expert_ids = lax.broadcasted_iota(jnp.int32, (rows, experts), 1)
    keep_float = keep_mask.astype(jnp.float32)
    keep_first, keep_second = keep_float[:, 0:1], keep_float[:, 1:2]
    hot_first = (expert_ids == routes[:, 0:1]).astype(jnp.float32)
    hot_second = (expert_ids == routes[:, 1:2]).astype(jnp.float32)
    gate_first = jnp.sum(probs * hot_first, axis=-1, keepdims=True) * keep_first
    gate_second = jnp.sum(probs * hot_second, axis=-1, keepdims=True) * keep_second
    columns = lax.broadcasted_iota(jnp.int32, (rows, slots), 1)
    target = routes * SLOTS + slot_index
    pick_first = (columns == target[:, 0:1]).astype(jnp.float32) * keep_first
    pick_second = (columns == target[:, 1:2]).astype(jnp.float32) * keep_second
    select = (pick_first + pick_second).astype(jnp.bfloat16)
    slot_gate = jnp.sum(pick_first * gate_first + pick_second * gate_second, axis=0)
    send_rows = product_t(select, normed).astype(jnp.bfloat16)
    send_grad = (product_t(select, grad_low) * slot_gate[:, None]).astype(jnp.bfloat16)
    def dispatch(rows_out):
        came = lax.all_to_all(
            rows_out.reshape(experts, SLOTS, width), ("z", "y"), split_axis=0, concat_axis=0, tiled=True
        ).reshape(slots, width)
        return jnp.concatenate([came, core_swap(came)], axis=0)

    flat, flat_grad = dispatch(send_rows), dispatch(send_grad)
    hidden, slope = gelu_parts(product_bt(flat, up_half))
    hidden = hidden.astype(jnp.bfloat16)
    partial_out = product(hidden, down_half)
    got_out = core_swap(partial_out[slots:].astype(jnp.bfloat16))
    pre_grad = (product_bt(flat_grad, down_half) * slope).astype(jnp.bfloat16)
    partial_in = product(pre_grad, up_half)
    got_in = core_swap(partial_in[slots:].astype(jnp.bfloat16))
    result = (partial_out[:slots] + got_out.astype(jnp.float32)).astype(jnp.bfloat16)
    in_grad = (partial_in[:slots] + got_in.astype(jnp.float32)).astype(jnp.bfloat16)
    back = jnp.concatenate(
        [result.reshape(experts, SLOTS, width), in_grad.reshape(experts, SLOTS, width)], axis=1
    )
    returned = lax.all_to_all(back, ("z", "y"), split_axis=0, concat_axis=0, tiled=True)
    result_rows = returned[:, :SLOTS].reshape(slots, width)
    back_rows = returned[:, SLOTS:].reshape(slots, width)

    down_low = product_t(hidden, flat_grad).astype(jnp.bfloat16)
    up_low = product_t(pre_grad, flat).astype(jnp.bfloat16)
    made = mark(down_low, up_low)
    down_grad = lax.psum_scatter(down_low, "x", scatter_dimension=0, tiled=True)
    up_grad = lax.psum_scatter(up_low, "x", scatter_dimension=0, tiled=True)
    down_grad = down_grad.astype(jnp.float32)
    up_grad = up_grad.astype(jnp.float32).T

    first = product(pick_first.astype(jnp.bfloat16), result_rows)
    second = product(pick_second.astype(jnp.bfloat16), result_rows)
    new_stream = stream + gate_first * first + gate_second * second
    gate_grad_first = jnp.sum(grad * first, axis=-1, keepdims=True) * keep_first
    gate_grad_second = jnp.sum(grad * second, axis=-1, keepdims=True) * keep_second
    probs_grad = gate_grad_first * hot_first + gate_grad_second * hot_second
    logit_grad = probs * (probs_grad - jnp.sum(probs * probs_grad, axis=-1, keepdims=True))
    logit_grad = logit_grad.astype(jnp.bfloat16)
    router_grad = product_t(normed, logit_grad)
    normed_grad = product_bt(logit_grad, router) + product(select, back_rows)
    stream_grad, gain_grad = norm_back(normed_grad, gain, saved)
    return (new_stream, grad + stream_grad, (gain_grad, router_grad, up_grad, down_grad), made)


def shards(
    tokens,
    norm_attn_a,
    in_proj_a,
    out_proj_a,
    norm_dense,
    dense_up,
    dense_down,
    norm_attn_b,
    in_proj_b,
    out_proj_b,
    norm_moe,
    router,
    expert_up,
    expert_down,
    routes,
    slot_index,
    keep_mask,
    output_grad,
):
    images, length, width = tokens.shape
    rows = images * length
    stream = tokens.reshape(rows, width).astype(jnp.float32)
    flat_routes = routes.reshape(rows, 2)
    flat_slots = slot_index.reshape(rows, 2)
    flat_keep = keep_mask.reshape(rows, 2)
    experts = router.shape[1]
    small = jnp.concatenate(
        [
            jnp.stack([norm_attn_a, norm_dense, norm_attn_b, norm_moe], axis=1),
            router,
            jnp.zeros((router.shape[0], 128 - 4 - experts), router.dtype),
        ],
        axis=1,
    )
    wide_in, wide_out = in_proj_a.shape[1], out_proj_a.shape[1]
    blocks, depth = X * CORES, in_proj_a.shape[0]
    every = slice(None)

    def side_by_side(widths):
        starts = [sum(widths[:at]) for at in range(len(widths))]
        return lambda spot: [
            ((every, pl.ds(start, wide)), at, (spot,))
            for at, (start, wide) in enumerate(zip(starts, widths))
        ]

    pieces = gather_pieces(jnp.concatenate([in_proj_a, out_proj_a, small], axis=1))
    widths = [wide_in, wide_out, 128]
    in_aa, out_aa, small_all = both_cores(
        pieces, [(blocks, depth, wide) for wide in widths], side_by_side(widths), len(widths)
    )
    in_aa, out_aa, small_all = (w.reshape(width, -1) for w in (in_aa, out_aa, small_all))
    gain_aa, gain_dd, gain_bb, gain_mm = (small_all[:, k] for k in range(4))
    router_full = small_all[:, 4 : 4 + experts]

    up_dd, down_dd = gather_dense(dense_up, dense_down)

    pieces = gather_pieces(jnp.concatenate([in_proj_b, out_proj_b], axis=1))
    widths = [wide_in, wide_out]
    in_bb, out_bb = both_cores(
        pieces, [(blocks, depth, wide) for wide in widths], side_by_side(widths), len(widths)
    )
    in_bb, out_bb = in_bb.reshape(width, -1), out_bb.reshape(width, -1)

    up_half = lax.all_gather(expert_up[0].T, "x", axis=0, tiled=True)
    down_half = lax.all_gather(expert_down[0], "x", axis=0, tiled=True)

    stream_one, kept_one = attend_forward(stream, gain_aa, in_aa, out_aa, images, length)
    stream_two, kept_two = dense_forward(stream_one, gain_dd, up_dd, down_dd)
    stream_three, kept_three = attend_forward(stream_two, gain_bb, in_bb, out_bb, images, length)
    stream_four, grad, moe_grads, made = moe(
        stream_three,
        output_grad.reshape(rows, width),
        gain_mm,
        router_full,
        up_half,
        down_half,
        flat_routes,
        flat_slots,
        flat_keep,
    )
    output = stream_four.astype(jnp.bfloat16).reshape(images, length, width)
    sent = mark(moe_grads[2], moe_grads[3])

    def late_product(left, right):
        return product_t(after(left, sent), right)

    grad = after(grad, made)
    grad, attn_b_grads = attend_backward(
        grad, gain_bb, in_bb, out_bb, kept_three, images, length, late_product
    )
    share_b = scatter_whole(jnp.concatenate(attn_b_grads[1:], axis=1))
    grad, dense_grads = dense_backward(grad, gain_dd, up_dd, down_dd, kept_two, sent)
    grad, attn_a_grads = attend_backward(
        grad, gain_aa, in_aa, out_aa, kept_one, images, length, weight_grad
    )
    input_grad = grad.reshape(images, length, width)
    small_grad = jnp.concatenate(
        [
            jnp.stack([attn_a_grads[0], dense_grads[0], attn_b_grads[0], moe_grads[0]], axis=0),
            moe_grads[1].T,
            jnp.zeros((128 - 4 - experts, width), jnp.float32),
        ],
        axis=0,
    )
    in_a, out_a, small_share = scatter_halves(
        *zip(attn_a_grads[1], attn_a_grads[2], split_rows(small_grad))
    )
    share_a = jnp.concatenate([in_a, out_a], axis=1)
    (share_a, share_b, down), small_total = sum_over_zy(
        [share_a, share_b, dense_grads[2]], small_share
    )
    (up,) = sum_over_zy([after(dense_grads[1], mark(share_a))], None)
    in_a, out_a = share_a[:, :wide_in], share_a[:, wide_in:]
    in_b, out_b = share_b[:, :wide_in], share_b[:, wide_in:]
    return (
        output,
        input_grad,
        small_total[:, 0],
        in_a,
        out_a,
        small_total[:, 1],
        up,
        down,
        small_total[:, 2],
        in_b,
        out_b,
        small_total[:, 3],
        small_total[:, 4 : 4 + experts],
        moe_grads[2][None],
        moe_grads[3][None],
    )


def solution(mesh):
    places = Mesh(mesh.devices.reshape(X, CORES, 4, 4), ("x", "core", "z", "y"))
    dp, expert = ("x", "core"), ("z", "y")
    images = P(dp + expert, None, None)
    return jax.shard_map(
        shards,
        mesh=places,
        in_specs=(
            images,
            P(dp),
            P(dp, None),
            P(dp, None),
            P(dp),
            P(dp, None),
            P(dp, None),
            P(dp),
            P(dp, None),
            P(dp, None),
            P(dp),
            P(dp, None),
            P(expert, None, dp),
            P(expert, dp, None),
            images,
            images,
            images,
            images,
        ),
        out_specs=(
            images,
            images,
            P(dp),
            P(dp, None),
            P(dp, None),
            P(dp),
            P(dp, None),
            P(dp, None),
            P(dp),
            P(dp, None),
            P(dp, None),
            P(dp),
            P(dp, None),
            P(expert, None, dp),
            P(expert, dp, None),
        ),
        check_vma=False,
    )
```
